256 devices in a mesh: section: 16 (over z_lo, y), dp: 2 (over core), tensor: 8 (over z_hi, x).
Axes of the slice: x: 4, y: 4, z: 8 (z_hi: 2, z_lo: 4; z = z_hi * 4 + z_lo), core: 2. Of those that a mesh axis runs over, the one named last changes fastest.
Arguments:
- partials: bfloat16 [16, 8, 256, 16384], P('section', 'tensor', 'dp'), parts along dimension 2, may hold values from -3 to 3
- residual: bfloat16 [16, 256, 16384], P('section', 'dp', 'tensor'), parts along dimension 1, may hold values from -48 to 48
- exponents: int32 [16, 256, 128], P('section', 'dp', 'tensor'), parts along dimension 1, may hold values from -8 to -4
- signs: int32 [16384], replicated, may hold values from 0 to 1
- gain: float32 [16384], replicated, may hold values from 0.1 to 1.9
- kv_weight: bfloat16 [16, 2, 16384, 1024], P('section', None, None, 'tensor'), may hold values from -0.046875 to 0.046875
Outputs:
- keys_values: bfloat16 [16, 2, 256, 1024], P('section', None, 'dp', 'tensor'), parts along dimension 2
The draws below stay inside these ranges and needn't reach their ends.
There are 2 independent parts, one for each index of `dp`. The reference program is written for one: setup_inputs(seed, part) draws one part's arguments, and reference() takes and returns one part's arrays. A program takes and returns all parts, laid end to end along the dimension named above; an argument that names none is the same for every part. Nothing has to cross between parts.
Inputs may be any that keep to these rules, and one draw needn't show every extreme that they name: `exponents`: scale exponent of each block of 128 features of a token. `signs`: sign bits, 1 for plus.
All inputs are finite; a program needn't handle non-finite values.
Results may differ from the reference program's by a relative error of at most 0.019.
Values may be sent and summed in bfloat16 or wider, within the bound.
A program may use at most 128 MiB of HBM per device.

```python
import math
import jax
import jax.numpy as jnp
from jax import lax

D = 16384
BLOCK = 128
TOK = 128
SECTIONS = 16
KV_COLS = 1024
N_TENSOR = 8


def draw_residual(key, part):
    key = jax.random.fold_in(key, 11)
    key_base, key_cols, key_rows = jax.random.split(key, 3)
    position = jnp.arange(D, dtype=jnp.float32) / D
    col_scale = jnp.power(3.0, position) * jnp.exp(jax.random.uniform(key_cols, (D,), jnp.float32, -0.69, 0.69))
    base = jax.random.truncated_normal(key_base, -4.0, 4.0, (SECTIONS, TOK, D), jnp.float32)
    rows = jnp.exp(jax.random.uniform(key_rows, (SECTIONS, TOK, 1), jnp.float32, -1.15, 1.15))
    value = base * rows * col_scale * 0.6
    return value.astype(jnp.bfloat16)


def plant(result, rng, least, high):
    index_at = [jax.random.randint(jax.random.fold_in(rng, axis), (), 0, length) for axis, length in enumerate(result.shape)]
    widest = result.shape.index(max(result.shape))
    neighbour = index_at[:widest] + [(index_at[widest] + 1) % result.shape[widest]] + index_at[widest + 1:]
    return result.at[tuple(index_at)].set(least).at[tuple(neighbour)].set(high)


def raised(values, key, source, target, blocks, factor):
    def block_of(dim):
        return (jnp.arange(values.shape[dim]) // (values.shape[dim] // blocks)).reshape((-1,) + (1,) * (values.ndim - 1 - dim))

    first = jax.random.permutation(key, blocks)[block_of(target)]
    second = (block_of(target) + blocks // 2) % blocks
    return jnp.where((block_of(source) == first) | (block_of(source) == second), factor * values, values)


def levels(rng, dims, pieces, smallest, high):
    level, own = 1.0, jax.random.fold_in(rng, 6)
    for dim, parts in pieces:
        draws = jnp.exp(jax.random.uniform(jax.random.fold_in(own, dim), (parts,), jnp.float32, smallest / len(pieces), high / len(pieces)))
        level = level * jnp.repeat(draws, dims[dim] // parts).reshape([-1 if axis == dim else 1 for axis in range(len(dims))])
    return level


def noise(stream_key, dims, deviation, bound, shards=(), held_as=jnp.bfloat16):
    values = deviation * jax.random.normal(stream_key, dims, jnp.float32)
    if shards:
        values = values * levels(stream_key, dims, shards, -0.22, 0.18)
    return jnp.clip(values, -bound, bound).astype(held_as)


def gaussian_with(key, dims, deviation, bound, pieces, heavy, kind=jnp.bfloat16):
    entries = deviation * jax.random.normal(key, dims, jnp.float32)
    if pieces:
        entries = entries * levels(key, dims, pieces, -0.22, 0.18)
    return jnp.clip(raised(entries, jax.random.fold_in(key, 3), *heavy), -bound, bound).astype(kind)


def setup_inputs(seed: int = 0, part: int = 0) -> dict:
    key_list = jax.random.split(jax.random.key(seed), 7)
    part_splits = jax.random.split(jax.random.fold_in(key_list[6], part), 7)
    partials = gaussian_with(part_splits[0], (SECTIONS, N_TENSOR, TOK, D), 0.5, 3.0, ((0, 16), (1, 8)), (1, 3, 8, 2.0))
    residual = draw_residual(jax.random.fold_in(jax.random.fold_in(key_list[6], part), 71), part)
    exponents = plant(jax.random.randint(part_splits[2], (SECTIONS, TOK, D // BLOCK), -8, -3), jax.random.fold_in(part_splits[2], 1), -8, (-3) - 1).astype(jnp.int32)
    signs = plant(jax.random.randint(key_list[3], (D,), 0, 2), jax.random.fold_in(key_list[3], 1), 0, 1).astype(jnp.int32)
    gain = jnp.clip(1.0 + 0.18 * jax.random.normal(key_list[4], (D,), jnp.float32), 0.1, 1.9)
    kv_weight = noise(key_list[5], (SECTIONS, 2, D, KV_COLS), D ** -0.5, 0.046875, ((0, 16), (3, 8)))
    return dict(partials=partials, residual=residual, exponents=exponents, signs=signs, gain=gain, kv_weight=kv_weight)


clip_level = 448.0
exp_low = -8
exp_high = -3
norm_eps = 1e-05

def rotation(order_size):
    rows_i = jnp.arange(order_size, dtype=jnp.int32)[:, None]
    cols_j = jnp.arange(order_size, dtype=jnp.int32)[None, :]
    parity = jnp.zeros((order_size, order_size), jnp.int32)
    level = 1
    while level < order_size:
        parity = parity + rows_i // level % 2 * (cols_j // level % 2)
        level = level * 2
    sign_h = (1 - 2 * (parity % 2)).astype(jnp.float32)
    return sign_h * jnp.float32(1.0 / math.sqrt(order_size))

def power_table(exponents_in, direction):
    factor = jnp.zeros(exponents_in.shape, jnp.float32)
    for power_level in range(exp_low, exp_high):
        factor = factor + jnp.where(exponents_in == power_level, jnp.float32(2.0 ** (direction * power_level)), jnp.float32(0.0))
    return factor

def encode(summed, exponents_in, sign_vals, matrix_h):
    rows_n, cols_n = summed.shape
    blk = matrix_h.shape[0]
    shaped = (summed * sign_vals).reshape(rows_n, cols_n // blk, blk)
    turned = jnp.einsum('tbk,kj->tbj', shaped, matrix_h, precision=lax.Precision.HIGHEST)
    scaled = turned * power_table(exponents_in, -1)[:, :, None]
    return jnp.clip(scaled, -clip_level, clip_level).astype(jnp.bfloat16).reshape(rows_n, cols_n)

def decode(coded, exponents_in, sign_vals, matrix_h):
    rows_n, cols_n = coded.shape
    blk = matrix_h.shape[0]
    shaped = coded.astype(jnp.float32).reshape(rows_n, cols_n // blk, blk) * power_table(exponents_in, 1)[:, :, None]
    turned = jnp.einsum('tbk,kj->tbj', shaped, matrix_h, precision=lax.Precision.HIGHEST)
    return turned.reshape(rows_n, cols_n) * sign_vals

def normalize(decoded, gain):
    meansq = lax.optimization_barrier(jnp.mean(decoded * decoded, axis=1, keepdims=True))
    return (decoded * lax.rsqrt(meansq + norm_eps) * gain).astype(jnp.bfloat16)

def reference(partials, residual, exponents, signs, gain, kv_weight):
    matrix_h = rotation(BLOCK)
    sign_all = (2 * signs - 1).astype(jnp.float32)

    def encode_section(items):
        part_now, resid_now, expo_now = items
        summed = resid_now.astype(jnp.float32) + lax.optimization_barrier(jnp.sum(part_now.astype(jnp.float32), axis=0))
        return encode(summed, expo_now, sign_all, matrix_h)
    coded = lax.map(encode_section, (partials, residual, exponents))
    got_coded = jnp.concatenate([jnp.zeros_like(coded[:1]), coded[:-1]], axis=0)
    got_expo = jnp.concatenate([jnp.zeros_like(exponents[:1]), exponents[:-1]], axis=0)

    def finish_section(items):
        coded_now, expo_now, weight_now = items
        normed = normalize(decode(coded_now, expo_now, sign_all, matrix_h), gain)
        product = jnp.einsum('td,cdh->cth', normed.astype(jnp.float32), weight_now.astype(jnp.float32))
        return product.astype(jnp.bfloat16)
    return lax.map(finish_section, (got_coded, got_expo, kv_weight))
```

```python
import functools
import math

import jax
import jax.numpy as jnp
from jax import lax
from jax.experimental import pallas as pl
from jax.experimental.pallas import tpu as pltpu
from jax.sharding import PartitionSpec as P

MESH = pl.DeviceIdType.MESH
BLOCK = 128
clip_level = 448.0
exp_low = -8
exp_high = -3
norm_eps = 1e-05
SLICES = 8
NX = 4


def power_table(exponents_in, direction):
    factor = jnp.zeros(exponents_in.shape, jnp.float32)
    for power_level in range(exp_low, exp_high):
        factor = factor + jnp.where(
            exponents_in == power_level,
            jnp.float32(2.0 ** (direction * power_level)),
            jnp.float32(0.0),
        )
    return factor


def hadamard_signs(rows, cols):
    i = lax.broadcasted_iota(jnp.int32, (rows, cols), 0)
    j = lax.broadcasted_iota(jnp.int32, (rows, cols), 1)
    p = (i & j) & (BLOCK - 1)
    p = p ^ (p >> 4)
    p = p ^ (p >> 2)
    p = p ^ (p >> 1)
    signs = (1 - 2 * (p & 1)).astype(jnp.float32)
    return jnp.where((i >> 7) == (j >> 7), signs, 0.0)


def kernel(
    part, resid, expo_h, signs_h, gain_h, w_h, out,
    pv, ab, rsb, zs, zr, ys, g, wv, wp, rv, expo, signs, gain, h_one, h_two, acc, ssq,
    pv_s, in_s, a_s, a_r, raw_s, comb_s, rs_r, z_s, z_r, y_s, y_r, ag_s, ag_r, fw_s, fw_r,
):
    n_sec = lax.axis_size("section")
    s, dp, t = lax.axis_index("section"), lax.axis_index("dp"), lax.axis_index("tensor")
    zh, x = t // NX, t % NX
    xr, xl, xo = (x + 1) % NX, (x + 3) % NX, (x + 2) % NX
    tok, slices, width = pv.shape[2], pv.shape[1], pv.shape[3]
    own = slices * width
    blocks = width // BLOCK
    norm_h = jnp.float32(1.0 / math.sqrt(BLOCK))

    def at(section, z_hi, col):
        return (section, dp, z_hi * NX + col)

    right, left, across = at(s, zh, xr), at(s, zh, xl), at(s, 1 - zh, x)

    def cols(z_hi, col, j):
        return pl.ds(pl.multiple_of((z_hi * NX + col) * own + j * width, width), width)

    own_loads = []
    for j in range(slices):
        for k, (z_hi, col) in enumerate(((0, xr), (1, xl), (0, x), (1, x))):
            own_loads.append(
                pltpu.make_async_copy(part.at[0, 0, :, cols(z_hi, col, j)], pv.at[k, j], pv_s.at[k, j])
            )
    small = [
        pltpu.make_async_copy(expo_h.at[0], expo, in_s.at[0]),
        pltpu.make_async_copy(signs_h, signs, in_s.at[1]),
        pltpu.make_async_copy(gain_h, gain, in_s.at[2]),
        pltpu.make_async_copy(resid.at[0], rv, in_s.at[3]),
        pltpu.make_async_copy(w_h.at[0, 0], wv.at[0], in_s.at[4]),
        pltpu.make_async_copy(w_h.at[0, 1], wv.at[1], in_s.at[5]),
    ]
    for c in own_loads[:8]:
        c.start()
    for c in small:
        c.start()
    for c in own_loads[8:]:
        c.start()

    bar = pltpu.get_barrier_semaphore()

    def greet(device):
        pl.semaphore_signal(bar, inc=1, device_id=device, device_id_type=MESH)

    for device in (right, left, across):
        greet(device)

    @pl.when(s > 0)
    def _():
        greet(at(s - 1, 0, x))
        greet(at(s - 1, 1, x))

    @pl.when(s < n_sec - 1)
    def _():
        greet(at(s + 1, 0, x))
        greet(at(s + 1, 1, x))

    before = (s + n_sec - 1) // n_sec
    after = (2 * n_sec - 2 - s) // n_sec
    pl.semaphore_wait(bar, 3 + 2 * before + 2 * after)

    def remote(src, dst, send, recv, device):
        return pltpu.make_async_remote_copy(
            src_ref=src, dst_ref=dst, send_sem=send, recv_sem=recv, device_id=device, device_id_type=MESH
        )

    def far(j, d):
        z_hi, device = (0, right) if d == 0 else (1, left)
        return remote(part.at[0, 0, :, cols(z_hi, xo, j)], ab.at[d, j], a_s.at[d, j], a_r.at[d, j], device)

    def near(j, d):
        z_hi, col, device = (1, xr, right) if d == 0 else (0, xl, left)
        return remote(
            part.at[0, 0, :, cols(z_hi, col, j)], rsb.at[z_hi, d, j], raw_s.at[d, j], rs_r.at[z_hi, d, j], device
        )

    def comb(j, d):
        device = right if d == 0 else left
        return remote(ab.at[d, j], rsb.at[d, d, j], comb_s.at[d, j], rs_r.at[d, d, j], device)

    def pair(j):
        return remote(zs.at[j], zr.at[j], z_s.at[j], z_r.at[j], across)

    def hand(j, z_hi):
        return remote(
            ys.at[j], g.at[x, j, zh], y_s.at[z_hi, j], y_r.at[zh, j], at(s + 1, z_hi, x)
        )

    def gather(j, d, z_hi):
        device = right if d == 0 else left
        return remote(g.at[x, j, z_hi], g.at[x, j, z_hi], ag_s.at[d, z_hi, j], ag_r.at[d, z_hi, j], device)

    def forward(j, d):
        device, col = (right, xl) if d == 0 else (left, xr)
        return remote(g.at[col, j, d], g.at[col, j, d], fw_s.at[d, j], fw_r.at[d, j], device)

    def got_gather(j, d, z_hi):
        col = xl if d == 0 else xr
        remote(g.at[col, j, z_hi], g.at[col, j, z_hi], ag_s.at[d, z_hi, j], ag_r.at[d, z_hi, j], right).wait_recv()

    def got_forward(j, d):
        remote(g.at[xo, j, d], g.at[xo, j, d], fw_s.at[d, j], fw_r.at[d, j], right).wait_recv()

    for d in (0, 1):
        far(0, d).start()
    for d in (0, 1):
        near(0, d).start()
    for d in (0, 1):
        far(1, d).start()

    h_one[...] = hadamard_signs(BLOCK, BLOCK)
    h_two[...] = hadamard_signs(2 * BLOCK, 2 * BLOCK).astype(jnp.bfloat16)
    acc[...] = jnp.zeros_like(acc)
    ssq[...] = jnp.zeros_like(ssq)

    @pl.when(s == 0)
    def _():
        g[x] = jnp.zeros(g.shape[1:], g.dtype)

    def combine(j):
        for d in (0, 1):
            own_loads[4 * j + d].wait()
            far(j, d).wait_recv()
            ab[d, j] = (ab[d, j].astype(jnp.float32) + pv[d, j].astype(jnp.float32)).astype(jnp.bfloat16)
            comb(j, d).start()

    def gathered_sum(j, z_hi):
        return (
            rsb[z_hi, 0, j].astype(jnp.float32)
            + rsb[z_hi, 1, j].astype(jnp.float32)
            + pv[2 + z_hi, j].astype(jnp.float32)
        )

    def exchange(j):
        own_loads[4 * j + 2].wait()
        own_loads[4 * j + 3].wait()
        for d in (0, 1):
            near(j, d).wait_recv()
            comb(j, d).wait_recv()
        zs[j] = gathered_sum(j, 1 - zh).astype(jnp.bfloat16)
        pair(j).start()

    def row(ref, b):
        return ref[pl.ds(b, 1), :]

    def encode(j):
        pair(j).wait_recv()
        summed = (
            gathered_sum(j, zh)
            + zr[j].astype(jnp.float32)
            + rv[:, j * width : (j + 1) * width].astype(jnp.float32)
        )
        e = expo[...]
        for q in range(0, blocks, 2):
            b = t * (own // BLOCK) + j * blocks + q
            sgn = jnp.concatenate([row(signs, b), row(signs, b + 1)], axis=1)
            sgn = (2 * sgn - 1).astype(jnp.float32)
            value = summed[:, q * BLOCK : (q + 2) * BLOCK] * sgn
            high = value.astype(jnp.bfloat16)
            rest = value - high.astype(jnp.float32)
            mid = rest.astype(jnp.bfloat16)
            low = (rest - mid.astype(jnp.float32)).astype(jnp.bfloat16)
            h = h_two[...]
            turned = (
                jnp.dot(low, h, preferred_element_type=jnp.float32)
                + jnp.dot(mid, h, preferred_element_type=jnp.float32)
                + jnp.dot(high, h, preferred_element_type=jnp.float32)
            ) * norm_h
            for r in (0, 1):
                k = j * blocks + q + r
                column = jnp.broadcast_to(e[:, k : k + 1], (tok, BLOCK))
                scaled = turned[:, r * BLOCK : (r + 1) * BLOCK] * power_table(column, -1)
                coded = jnp.clip(scaled, -clip_level, clip_level).astype(jnp.bfloat16)
                ys[j, :, (q + r) * BLOCK : (q + r + 1) * BLOCK] = (
                    coded.astype(jnp.float32) * power_table(column, 1)
                ).astype(jnp.bfloat16)

        @pl.when(s < n_sec - 1)
        def _():
            for z_hi in (0, 1):
                hand(j, z_hi).start()

    def fold_weights(j):
        def body(i, carry):
            b = (i // blocks) * (own // BLOCK) + j * blocks + i % blocks
            scale = (2 * row(signs, b) - 1).astype(jnp.float32) * row(gain, b)
            turn = h_one[...] * scale
            high = turn.astype(jnp.bfloat16)
            low = (turn - high.astype(jnp.float32)).astype(jnp.bfloat16)
            rows = pl.ds(pl.multiple_of(b * BLOCK, BLOCK), BLOCK)
            w = jnp.concatenate([wv[0, rows, :], wv[1, rows, :]], axis=1)
            prod = jnp.dot(
                jnp.concatenate([high, low], axis=1),
                jnp.concatenate([w, w], axis=0),
                preferred_element_type=jnp.float32,
            )
            wp[rows, :] = (prod * norm_h).astype(jnp.bfloat16)
            return carry

        lax.fori_loop(0, 2 * NX * blocks, body, 0, unroll=2)

    def spread(j):
        @pl.when(s > 0)
        def _():
            for z_hi in (0, 1):
                remote(ys.at[j], g.at[x, j, z_hi], y_s.at[z_hi, j], y_r.at[z_hi, j], right).wait_recv()

        for d, z_hi in ((0, 0), (1, 1), (0, 1), (1, 0)):
            gather(j, d, z_hi).start()

    def pass_on(j):
        for d in (0, 1):
            got_gather(j, d, d)
            forward(j, d).start()

    def project(j, col, z_hi):
        v = g[col, j, z_hi]
        rows = pl.ds(pl.multiple_of((z_hi * NX + col) * own + j * width, width), width)
        acc[...] += jnp.dot(v, wp[rows, :], preferred_element_type=jnp.float32)
        f = v.astype(jnp.float32)
        sq = f * f
        total = sq[:, :BLOCK]
        for q in range(1, blocks):
            total = total + sq[:, q * BLOCK : (q + 1) * BLOCK]
        ssq[...] += total

    for k in range(slices):
        combine(k)
        if k + 1 < slices:
            for d in (0, 1):
                near(k + 1, d).start()
        if k + 2 < slices:
            for d in (0, 1):
                far(k + 2, d).start()
        if k == 0:
            for c in small:
                c.wait()
        fold_weights(k)
        if k >= 1:
            exchange(k - 1)
        if k >= 3:
            encode(k - 3)

    spread(0)
    spread(1)
    exchange(slices - 1)
    for k in range(slices):
        if k < 3:
            encode(slices - 3 + k)
        if k + 2 < slices:
            spread(k + 2)
        pass_on(k)
        project(k, x, 0)
        project(k, x, 1)
        project(k, xl, 0)
        project(k, xr, 1)
        got_gather(k, 0, 1)
        project(k, xl, 1)
        got_gather(k, 1, 0)
        project(k, xr, 0)
        if k >= 1:
            for d in (0, 1):
                got_forward(k - 1, d)
                project(k - 1, xo, d)
        for d in (0, 1):
            far(k, d).wait_send()
            near(k, d).wait_send()
            comb(k, d).wait_send()
        if k >= 1:
            pair(k - 1).wait_send()
            for d in (0, 1):
                forward(k - 1, d).wait_send()
                for z_hi in (0, 1):
                    gather(k - 1, d, z_hi).wait_send()
        if k == slices - 1:
            pair(k).wait_send()

            @pl.when(s < n_sec - 1)
            def _():
                for j in range(slices):
                    for z_hi in (0, 1):
                        hand(j, z_hi).wait_send()

    last = slices - 1
    for d in (0, 1):
        got_forward(last, d)
        project(last, xo, d)
    mean = jnp.sum(ssq[...], axis=1, keepdims=True) * jnp.float32(1.0 / (2 * NX * own))
    result = acc[...] * lax.rsqrt(mean + norm_eps)
    out[0, 0] = result[:, :BLOCK].astype(out.dtype)
    out[0, 1] = result[:, BLOCK:].astype(out.dtype)
    for d in (0, 1):
        forward(last, d).wait_send()
        for z_hi in (0, 1):
            gather(last, d, z_hi).wait_send()


def on_device(partials, residual, exponents, signs, gain, kv_weight):
    tok, own = residual.shape[1], residual.shape[2]
    model = signs.shape[0]
    c = SLICES
    width = own // c
    bf, f32 = jnp.bfloat16, jnp.float32
    dma = pltpu.SemaphoreType.DMA
    blocks2d = (model // BLOCK, BLOCK)
    return pl.pallas_call(
        kernel,
        out_shape=jax.ShapeDtypeStruct((1, 2, tok, kv_weight.shape[3]), bf),
        in_specs=[pl.BlockSpec(memory_space=pl.ANY)] * 6,
        out_specs=pl.BlockSpec(memory_space=pltpu.VMEM),
        scratch_shapes=[
            pltpu.VMEM((4, c, tok, width), bf),
            pltpu.VMEM((2, c, tok, width), bf),
            pltpu.VMEM((2, 2, c, tok, width), bf),
            pltpu.VMEM((c, tok, width), bf),
            pltpu.VMEM((c, tok, width), bf),
            pltpu.VMEM((c, tok, width), bf),
            pltpu.VMEM((NX, c, 2, tok, width), bf),
            pltpu.VMEM((2, model, BLOCK), bf),
            pltpu.VMEM((model, 2 * BLOCK), bf),
            pltpu.VMEM((tok, own), bf),
            pltpu.VMEM((tok, own // BLOCK), jnp.int32),
            pltpu.VMEM(blocks2d, jnp.int32),
            pltpu.VMEM(blocks2d, f32),
            pltpu.VMEM((BLOCK, BLOCK), f32),
            pltpu.VMEM((2 * BLOCK, 2 * BLOCK), bf),
            pltpu.VMEM((tok, 2 * BLOCK), f32),
            pltpu.VMEM((tok, BLOCK), f32),
            dma((4, c)),
            dma((6,)),
            dma((2, c)),
            dma((2, c)),
            dma((2, c)),
            dma((2, c)),
            dma((2, 2, c)),
            dma((c,)),
            dma((c,)),
            dma((2, c)),
            dma((2, c)),
            dma((2, 2, c)),
            dma((2, 2, c)),
            dma((2, c)),
            dma((2, c)),
        ],
        compiler_params=pltpu.CompilerParams(
            collective_id=0, has_side_effects=True, vmem_limit_bytes=48 << 20
        ),
        cost_estimate=pl.CostEstimate(
            flops=6 * tok * model * 2 * BLOCK, bytes_accessed=14 << 20, transcendentals=tok
        ),
        name="relay",
    )(partials, residual, exponents, signs.reshape(blocks2d), gain.reshape(blocks2d), kv_weight)


def solution(mesh):
    placed = (
        P("section", "tensor", "dp", None),
        P("section", "dp", "tensor"),
        P("section", "dp", "tensor"),
        P(),
        P(),
        P("section", None, None, "tensor"),
    )
    return jax.shard_map(
        on_device,
        mesh=mesh,
        in_specs=placed,
        out_specs=P("section", None, "dp", "tensor"),
        check_vma=False,
    )
```

```python
import functools
import math

import jax
import jax.numpy as jnp
from jax import lax
from jax.experimental import pallas as pl
from jax.experimental.pallas import tpu as pltpu
from jax.sharding import PartitionSpec as P

MESH = pl.DeviceIdType.MESH
BLOCK = 128
clip_level = 448.0
exp_low = -8
exp_high = -3
norm_eps = 1e-05
SLICES = 8
TAIL = (
    "S0", "S1", "X7", "S2", "E5", "P0", "S3", "E6", "R0", "R1", "P1", "S4", "E7", "R2",
    "P2", "R3", "S5", "P3", "R4", "N0", "S6", "P4", "N1", "R5", "S7", "P5", "R6", "N2",
    "R7", "P6", "N3", "O0", "P7", "N4", "F0", "F1", "O1", "N5", "F2", "F3", "O2", "N6",
    "F4", "Q0", "N7", "F5", "O3", "Q1", "F6", "F7", "M0", "O4", "Q2", "M1", "G0", "O5",
    "Q3", "M2", "G1", "O6", "Q4", "M3", "G2", "O7", "Q5", "M4", "G3", "Q6", "M5", "G4",
    "Q7", "M6", "G5", "M7", "G6", "G7",
)
NX = 4


def power_table(exponents_in, direction):
    factor = jnp.zeros(exponents_in.shape, jnp.float32)
    for power_level in range(exp_low, exp_high):
        factor = factor + jnp.where(
            exponents_in == power_level,
            jnp.float32(2.0 ** (direction * power_level)),
            jnp.float32(0.0),
        )
    return factor


def hadamard_signs(rows, cols):
    i = lax.broadcasted_iota(jnp.int32, (rows, cols), 0)
    j = lax.broadcasted_iota(jnp.int32, (rows, cols), 1)
    p = (i & j) & (BLOCK - 1)
    p = p ^ (p >> 4)
    p = p ^ (p >> 2)
    p = p ^ (p >> 1)
    signs = (1 - 2 * (p & 1)).astype(jnp.float32)
    return jnp.where((i >> 7) == (j >> 7), signs, 0.0)


def kernel(
    part, resid, expo_h, signs_h, gain_h, w_h, out,
    pv, ab, rsb, zs, zr, ys, g, wv, wp, rv, expo, signs, gain, h_one, h_two, acc, ssq,
    pv_s, in_s, a_s, a_r, raw_s, comb_s, rs_r, z_s, z_r, y_s, y_r, c_s, ag_s, ag_r, fw_s, fw_r,
):
    n_sec = lax.axis_size("section")
    s, dp, t = lax.axis_index("section"), lax.axis_index("dp"), lax.axis_index("tensor")
    zh, x = t // NX, t % NX
    xr, xl, xo = (x + 1) % NX, (x + 3) % NX, (x + 2) % NX
    tok, slices, width = pv.shape[2], pv.shape[1], pv.shape[3]
    own = slices * width
    blocks = width // BLOCK
    norm_h = jnp.float32(1.0 / math.sqrt(BLOCK))

    def at(section, z_hi, col):
        return (section, dp, z_hi * NX + col)

    right, left, across = at(s, zh, xr), at(s, zh, xl), at(s, 1 - zh, x)

    def cols(z_hi, col, j):
        return pl.ds(pl.multiple_of((z_hi * NX + col) * own + j * width, width), width)

    own_loads = []
    for j in range(slices):
        for k, (z_hi, col) in enumerate(((0, xr), (1, xl), (0, x), (1, x))):
            own_loads.append(
                pltpu.make_async_copy(part.at[0, 0, :, cols(z_hi, col, j)], pv.at[k, j], pv_s.at[k, j])
            )
    small = [
        pltpu.make_async_copy(expo_h.at[0], expo, in_s.at[0]),
        pltpu.make_async_copy(signs_h, signs, in_s.at[1]),
        pltpu.make_async_copy(gain_h, gain, in_s.at[2]),
        pltpu.make_async_copy(resid.at[0], rv, in_s.at[3]),
        pltpu.make_async_copy(w_h.at[0, 0], wv.at[0], in_s.at[4]),
        pltpu.make_async_copy(w_h.at[0, 1], wv.at[1], in_s.at[5]),
    ]
    for c in own_loads[:8]:
        c.start()
    for c in small:
        c.start()
    for c in own_loads[8:]:
        c.start()

    bar = pltpu.get_barrier_semaphore()

    def greet(device):
        pl.semaphore_signal(bar, inc=1, device_id=device, device_id_type=MESH)

    for device in (right, left, across):
        greet(device)

    @pl.when(s > 0)
    def _():
        greet(at(s - 1, zh, x))

    @pl.when(s < n_sec - 1)
    def _():
        greet(at(s + 1, zh, x))

    before = (s + n_sec - 1) // n_sec
    after = (2 * n_sec - 2 - s) // n_sec
    pl.semaphore_wait(bar, 3 + before + after)

    def remote(src, dst, send, recv, device):
        return pltpu.make_async_remote_copy(
            src_ref=src, dst_ref=dst, send_sem=send, recv_sem=recv, device_id=device, device_id_type=MESH
        )

    def far(j, d):
        z_hi, device = (0, right) if d == 0 else (1, left)
        return remote(part.at[0, 0, :, cols(z_hi, xo, j)], ab.at[d, j], a_s.at[d, j], a_r.at[d, j], device)

    def near(j, d):
        z_hi, col, device = (1, xr, right) if d == 0 else (0, xl, left)
        return remote(
            part.at[0, 0, :, cols(z_hi, col, j)], rsb.at[z_hi, d, j], raw_s.at[d, j], rs_r.at[z_hi, d, j], device
        )

    def comb(j, d):
        device = right if d == 0 else left
        return remote(ab.at[d, j], rsb.at[d, d, j], comb_s.at[d, j], rs_r.at[d, d, j], device)

    def pair(j):
        return remote(zs.at[j], zr.at[j], z_s.at[j], z_r.at[j], across)

    def hand(j):
        return remote(ys.at[j], g.at[x, j, zh], y_s.at[j], y_r.at[zh, j], at(s + 1, zh, x))

    def relay_across(j):
        return remote(g.at[x, j, zh], g.at[x, j, zh], c_s.at[j], y_r.at[zh, j], across)

    def gather(j, d, z_hi):
        device = right if d == 0 else left
        return remote(g.at[x, j, z_hi], g.at[x, j, z_hi], ag_s.at[d, z_hi, j], ag_r.at[d, z_hi, j], device)

    def onward(j, z_hi):
        d = (z_hi + j) % 2
        return d, (x + 3 + 2 * d) % NX, at(s, zh, (x + 1 + 2 * d) % NX)

    def forward(j, z_hi):
        d, col, device = onward(j, z_hi)
        return remote(g.at[col, j, z_hi], g.at[col, j, z_hi], fw_s.at[z_hi, j], fw_r.at[z_hi, j], device)

    def got_gather(j, d, z_hi):
        col = (x + 3 + 2 * d) % NX
        remote(g.at[col, j, z_hi], g.at[col, j, z_hi], ag_s.at[d, z_hi, j], ag_r.at[d, z_hi, j], right).wait_recv()

    def got_forward(j, z_hi):
        remote(g.at[xo, j, z_hi], g.at[xo, j, z_hi], fw_s.at[z_hi, j], fw_r.at[z_hi, j], right).wait_recv()

    for d in (0, 1):
        far(0, d).start()
    for d in (0, 1):
        near(0, d).start()
    for d in (0, 1):
        far(1, d).start()

    h_one[...] = hadamard_signs(BLOCK, BLOCK)
    h_two[...] = hadamard_signs(2 * BLOCK, 2 * BLOCK).astype(jnp.bfloat16)
    acc[...] = jnp.zeros_like(acc)
    ssq[...] = jnp.zeros_like(ssq)

    @pl.when(s == 0)
    def _():
        g[x] = jnp.zeros(g.shape[1:], g.dtype)

    def combine(j):
        for d in (0, 1):
            own_loads[4 * j + d].wait()
            far(j, d).wait_recv()
            ab[d, j] = (ab[d, j].astype(jnp.float32) + pv[d, j].astype(jnp.float32)).astype(jnp.bfloat16)
            comb(j, d).start()

    def gathered_sum(j, z_hi):
        return (
            rsb[z_hi, 0, j].astype(jnp.float32)
            + rsb[z_hi, 1, j].astype(jnp.float32)
            + pv[2 + z_hi, j].astype(jnp.float32)
        )

    def exchange(j):
        own_loads[4 * j + 2].wait()
        own_loads[4 * j + 3].wait()
        for d in (0, 1):
            near(j, d).wait_recv()
            comb(j, d).wait_recv()
        zs[j] = gathered_sum(j, 1 - zh).astype(jnp.bfloat16)
        pair(j).start()

    def row(ref, b):
        return ref[pl.ds(b, 1), :]

    def encode(j):
        pair(j).wait_recv()
        summed = (
            gathered_sum(j, zh)
            + zr[j].astype(jnp.float32)
            + rv[:, j * width : (j + 1) * width].astype(jnp.float32)
        )
        e = jnp.swapaxes(expo[...], 0, 1)
        for q in range(0, blocks, 2):
            b = t * (own // BLOCK) + j * blocks + q
            sgn = jnp.concatenate([row(signs, b), row(signs, b + 1)], axis=1)
            sgn = (2 * sgn - 1).astype(jnp.float32)
            value = summed[:, q * BLOCK : (q + 2) * BLOCK] * sgn
            high = value.astype(jnp.bfloat16)
            rest = value - high.astype(jnp.float32)
            mid = rest.astype(jnp.bfloat16)
            low = (rest - mid.astype(jnp.float32)).astype(jnp.bfloat16)
            h = h_two[...]
            turned = (
                jnp.dot(low, h, preferred_element_type=jnp.float32)
                + jnp.dot(mid, h, preferred_element_type=jnp.float32)
                + jnp.dot(high, h, preferred_element_type=jnp.float32)
            ) * norm_h
            for r in (0, 1):
                k = j * blocks + q + r
                column = jnp.broadcast_to(e[:, k : k + 1], (tok, BLOCK))
                scaled = turned[:, r * BLOCK : (r + 1) * BLOCK] * power_table(column, -1)
                coded = jnp.clip(scaled, -clip_level, clip_level).astype(jnp.bfloat16)
                ys[j, :, (q + r) * BLOCK : (q + r + 1) * BLOCK] = (
                    coded.astype(jnp.float32) * power_table(column, 1)
                ).astype(jnp.bfloat16)

        @pl.when(s < n_sec - 1)
        def _():
            hand(j).start()

    def fold_weights(j):
        def body(i, carry):
            b = (i // blocks) * (own // BLOCK) + j * blocks + i % blocks
            scale = (2 * row(signs, b) - 1).astype(jnp.float32) * row(gain, b)
            turn = h_one[...] * scale
            high = turn.astype(jnp.bfloat16)
            low = (turn - high.astype(jnp.float32)).astype(jnp.bfloat16)
            rows = pl.ds(pl.multiple_of(b * BLOCK, BLOCK), BLOCK)
            w = jnp.concatenate([wv[0, rows, :], wv[1, rows, :]], axis=1)
            prod = jnp.dot(
                jnp.concatenate([high, low], axis=1),
                jnp.concatenate([w, w], axis=0),
                preferred_element_type=jnp.float32,
            )
            wp[rows, :] = (prod * norm_h).astype(jnp.bfloat16)
            return carry

        lax.fori_loop(0, 2 * NX * blocks, body, 0, unroll=2)

    def arrived(j, z_hi):
        remote(g.at[x, j, z_hi], g.at[x, j, z_hi], c_s.at[j], y_r.at[z_hi, j], right).wait_recv()

    def relay(j):
        @pl.when(s > 0)
        def _():
            relay_across(j).start()

    def spread(j):
        @pl.when(s > 0)
        def _():
            arrived(j, zh)

        for d in (0, 1):
            gather(j, d, zh).start()

    def spread_other(j):
        @pl.when(s > 0)
        def _():
            arrived(j, 1 - zh)

        for d in (0, 1):
            gather(j, d, 1 - zh).start()

    def pass_on(j, z_hi):
        d, _, _ = onward(j, z_hi)
        got_gather(j, d, z_hi)
        forward(j, z_hi).start()

    def project(j, col, z_hi):
        v = g[col, j, z_hi]
        rows = pl.ds(pl.multiple_of((z_hi * NX + col) * own + j * width, width), width)
        acc[...] += jnp.dot(v, wp[rows, :], preferred_element_type=jnp.float32)
        f = v.astype(jnp.float32)
        sq = f * f
        total = sq[:, :BLOCK]
        for q in range(1, blocks):
            total = total + sq[:, q * BLOCK : (q + 1) * BLOCK]
        ssq[...] += total

    def send_on(j):
        if j < slices:
            for d in (0, 1):
                near(j, d).start()
        if j + 1 < slices:
            for d in (0, 1):
                far(j + 1, d).start()

    def project_near(j, z_hi):
        d, col, _ = onward(j, z_hi)
        project(j, x, z_hi)
        project(j, col, z_hi)
        got_gather(j, 1 - d, z_hi)
        project(j, (x + 1 + 2 * d) % NX, z_hi)

    def project_far(j, z_hi):
        got_forward(j, z_hi)
        project(j, xo, z_hi)

    def sent_sums(k):
        for d in (0, 1):
            far(k, d).wait_send()
            near(k, d).wait_send()
            comb(k, d).wait_send()
        pair(k).wait_send()

    def sent_gather(j, z_hi):
        forward(j, z_hi).wait_send()
        for d in (0, 1):
            gather(j, d, z_hi).wait_send()

    for k in range(slices):
        combine(k)
        send_on(k + 1)
        if k == 0:
            for c in small:
                c.wait()
        fold_weights(k)
        if k >= 1:
            exchange(k - 1)
        if k >= 3:
            encode(k - 3)

    for step in TAIL:
        kind, k = step[0], int(step[1:])
        if kind == "X":
            exchange(k)
        elif kind == "E":
            encode(k)
        elif kind == "R":
            relay(k)
        elif kind == "S":
            spread(k)
        elif kind == "O":
            spread_other(k)
        elif kind in "PQ":
            pass_on(k, zh if kind == "P" else 1 - zh)
        elif kind in "NM":
            project_near(k, zh if kind == "N" else 1 - zh)
            if kind == "N":
                sent_sums(k)
        elif kind in "FG":
            z_hi = zh if kind == "F" else 1 - zh
            project_far(k, z_hi)
            sent_gather(k, z_hi)

    @pl.when(s < n_sec - 1)
    def _():
        for j in range(slices):
            hand(j).wait_send()

    @pl.when(s > 0)
    def _():
        for j in range(slices):
            relay_across(j).wait_send()

    mean = jnp.sum(ssq[...], axis=1, keepdims=True) * jnp.float32(1.0 / (2 * NX * own))
    result = acc[...] * lax.rsqrt(mean + norm_eps)
    out[0, 0] = result[:, :BLOCK].astype(out.dtype)
    out[0, 1] = result[:, BLOCK:].astype(out.dtype)


def on_device(partials, residual, exponents, signs, gain, kv_weight):
    tok, own = residual.shape[1], residual.shape[2]
    model = signs.shape[0]
    c = SLICES
    width = own // c
    bf, f32 = jnp.bfloat16, jnp.float32
    dma = pltpu.SemaphoreType.DMA
    blocks2d = (model // BLOCK, BLOCK)
    return pl.pallas_call(
        kernel,
        out_shape=jax.ShapeDtypeStruct((1, 2, tok, kv_weight.shape[3]), bf),
        in_specs=[pl.BlockSpec(memory_space=pl.ANY)] * 6,
        out_specs=pl.BlockSpec(memory_space=pltpu.VMEM),
        scratch_shapes=[
            pltpu.VMEM((4, c, tok, width), bf),
            pltpu.VMEM((2, c, tok, width), bf),
            pltpu.VMEM((2, 2, c, tok, width), bf),
            pltpu.VMEM((c, tok, width), bf),
            pltpu.VMEM((c, tok, width), bf),
            pltpu.VMEM((c, tok, width), bf),
            pltpu.VMEM((NX, c, 2, tok, width), bf),
            pltpu.VMEM((2, model, BLOCK), bf),
            pltpu.VMEM((model, 2 * BLOCK), bf),
            pltpu.VMEM((tok, own), bf),
            pltpu.VMEM((own // BLOCK, tok), jnp.int32),
            pltpu.VMEM(blocks2d, jnp.int32),
            pltpu.VMEM(blocks2d, f32),
            pltpu.VMEM((BLOCK, BLOCK), f32),
            pltpu.VMEM((2 * BLOCK, 2 * BLOCK), bf),
            pltpu.VMEM((tok, 2 * BLOCK), f32),
            pltpu.VMEM((tok, BLOCK), f32),
            dma((4, c)),
            dma((6,)),
            dma((2, c)),
            dma((2, c)),
            dma((2, c)),
            dma((2, c)),
            dma((2, 2, c)),
            dma((c,)),
            dma((c,)),
            dma((c,)),
            dma((2, c)),
            dma((c,)),
            dma((2, 2, c)),
            dma((2, 2, c)),
            dma((2, c)),
            dma((2, c)),
        ],
        compiler_params=pltpu.CompilerParams(
            collective_id=0, has_side_effects=True, vmem_limit_bytes=62 << 20
        ),
        cost_estimate=pl.CostEstimate(
            flops=6 * tok * model * 2 * BLOCK, bytes_accessed=14 << 20, transcendentals=tok
        ),
        name="relay",
    )(partials, residual, jnp.swapaxes(exponents, 1, 2), signs.reshape(blocks2d), gain.reshape(blocks2d), kv_weight)


def solution(mesh):
    placed = (
        P("section", "tensor", "dp", None),
        P("section", "dp", "tensor"),
        P("section", "dp", "tensor"),
        P(),
        P(),
        P("section", None, None, "tensor"),
    )
    return jax.shard_map(
        on_device,
        mesh=mesh,
        in_specs=placed,
        out_specs=P("section", None, "dp", "tensor"),
        check_vma=False,
    )
```

```python
import functools
import math

import jax
import jax.numpy as jnp
from jax import lax
from jax.experimental import pallas as pl
from jax.experimental.pallas import tpu as pltpu
from jax.sharding import PartitionSpec as P

MESH = pl.DeviceIdType.MESH
BLOCK = 128
clip_level = 448.0
exp_low = -8
exp_high = -3
norm_eps = 1e-05
SLICES = 8
TAIL = (
    "S2", "D3", "S3", "X7", "E5", "P0", "P1", "E6", "S4", "R0", "P2", "D5", "S5", "R1",
    "E7", "P3", "S6", "R2", "N0", "P4", "D7", "S7", "R3", "N1", "P5", "R4", "N2", "R5",
    "P6", "N3", "R6", "O0", "P7", "R7", "N4", "F0", "F1", "O1", "N5", "F2", "F3", "O2",
    "N6", "F4", "Q0", "N7", "F5", "O3", "Q1", "F6", "F7", "M0", "O4", "Q2", "M1", "G0",
    "O5", "Q3", "M2", "G1", "O6", "Q4", "M3", "G2", "O7", "Q5", "M4", "G3", "Q6", "M5",
    "G4", "Q7", "M6", "G5", "M7", "G6", "G7",
)
NX = 4
NY = 4


def power_table(exponents_in, direction):
    factor = jnp.zeros(exponents_in.shape, jnp.float32)
    for power_level in range(exp_low, exp_high):
        factor = factor + jnp.where(
            exponents_in == power_level,
            jnp.float32(2.0 ** (direction * power_level)),
            jnp.float32(0.0),
        )
    return factor


def hadamard_signs(rows, cols):
    i = lax.broadcasted_iota(jnp.int32, (rows, cols), 0)
    j = lax.broadcasted_iota(jnp.int32, (rows, cols), 1)
    p = (i & j) & (BLOCK - 1)
    p = p ^ (p >> 4)
    p = p ^ (p >> 2)
    p = p ^ (p >> 1)
    signs = (1 - 2 * (p & 1)).astype(jnp.float32)
    return jnp.where((i >> 7) == (j >> 7), signs, 0.0)


def kernel(
    part, resid, expo_h, signs_h, gain_h, w_h, out,
    pv, ab, rsb, zs, zr, ys, rb, g, wv, wp, rv, expo, signs, gain, h_one, h_two, acc, ssq,
    pv_s, in_s, a_s, a_r, raw_s, comb_s, rs_r, z_s, z_r, y_s, y_r, c_s, d_s, d_r, ag_s, ag_r, fw_s, fw_r,
):
    n_sec = lax.axis_size("section")
    s, dp, t = lax.axis_index("section"), lax.axis_index("dp"), lax.axis_index("tensor")
    zh, x = t // NX, t % NX
    xr, xl, xo = (x + 1) % NX, (x + 3) % NX, (x + 2) % NX
    tok, slices, width = pv.shape[2], pv.shape[1], pv.shape[3]
    own = slices * width
    blocks = width // BLOCK
    closing = (s % NY) // (NY - 1) * ((2 * n_sec - 2 - s) // n_sec)
    first = 1 - (s % NY + NY - 1) // NY
    between = first * (1 - s // (n_sec - NY))
    opening = first * ((s + n_sec - 1) // n_sec)
    norm_h = jnp.float32(1.0 / math.sqrt(BLOCK))

    def at(section, z_hi, col):
        return (section, dp, z_hi * NX + col)

    right, left, across = at(s, zh, xr), at(s, zh, xl), at(s, 1 - zh, x)

    def cols(z_hi, col, j):
        return pl.ds(pl.multiple_of((z_hi * NX + col) * own + j * width, width), width)

    own_loads = []
    for j in range(slices):
        for k, (z_hi, col) in enumerate(((0, xr), (1, xl), (0, x), (1, x))):
            own_loads.append(
                pltpu.make_async_copy(part.at[0, 0, :, cols(z_hi, col, j)], pv.at[k, j], pv_s.at[k, j])
            )
    small = [
        pltpu.make_async_copy(expo_h.at[0], expo, in_s.at[0]),
        pltpu.make_async_copy(signs_h, signs, in_s.at[1]),
        pltpu.make_async_copy(gain_h, gain, in_s.at[2]),
        pltpu.make_async_copy(resid.at[0], rv, in_s.at[3]),
        pltpu.make_async_copy(w_h.at[0, 0], wv.at[0], in_s.at[4]),
        pltpu.make_async_copy(w_h.at[0, 1], wv.at[1], in_s.at[5]),
    ]
    bar = pltpu.get_barrier_semaphore()

    def greet(device):
        pl.semaphore_signal(bar, inc=1, device_id=device, device_id_type=MESH)

    for device in (right, left, across):
        greet(device)

    @pl.when(s > 0)
    def _():
        greet(at(s - 1, zh, x))

    @pl.when(s < n_sec - 1)
    def _():
        greet(at(s + 1, zh, x))

    @pl.when(closing == 1)
    def _():
        greet(at(s - (NY - 1), zh, x))

    @pl.when(between == 1)
    def _():
        greet(at(s + NY - 1, zh, x))
        greet(at(s + NY, zh, x))

    @pl.when(opening == 1)
    def _():
        greet(at(s - NY, zh, x))

    before = (s + n_sec - 1) // n_sec
    after = (2 * n_sec - 2 - s) // n_sec
    for c in own_loads[:8]:
        c.start()
    pl.semaphore_wait(bar, 3 + before + after + closing + 2 * between + opening)

    def remote(src, dst, send, recv, device):
        return pltpu.make_async_remote_copy(
            src_ref=src, dst_ref=dst, send_sem=send, recv_sem=recv, device_id=device, device_id_type=MESH
        )

    def far(j, d):
        z_hi, device = (0, right) if d == 0 else (1, left)
        return remote(part.at[0, 0, :, cols(z_hi, xo, j)], ab.at[d, j], a_s.at[d, j], a_r.at[d, j], device)

    def near(j, d):
        z_hi, col, device = (1, xr, right) if d == 0 else (0, xl, left)
        return remote(
            part.at[0, 0, :, cols(z_hi, col, j)], rsb.at[z_hi, d, j], raw_s.at[d, j], rs_r.at[z_hi, d, j], device
        )

    def comb(j, d):
        device = right if d == 0 else left
        return remote(ab.at[d, j], rsb.at[d, d, j], comb_s.at[d, j], rs_r.at[d, d, j], device)

    def pair(j):
        return remote(zs.at[j], zr.at[j], z_s.at[j], z_r.at[j], across)

    def hand(j):
        return remote(ys.at[j], g.at[x, j, zh], y_s.at[j], y_r.at[zh, j], at(s + 1, zh, x))

    def detour(j):
        return remote(ys.at[j], rb.at[j // 2], y_s.at[j], d_r.at[j // 2], at(s - (NY - 1), zh, x))

    def detour_on(j):
        return remote(rb.at[j // 2], g.at[x, j, zh], d_s.at[j // 2], y_r.at[zh, j], at(s + NY, zh, x))

    def relay_across(j):
        return remote(g.at[x, j, zh], g.at[x, j, zh], c_s.at[j], y_r.at[zh, j], across)

    def gather(j, d, z_hi):
        device = right if d == 0 else left
        return remote(g.at[x, j, z_hi], g.at[x, j, z_hi], ag_s.at[d, z_hi, j], ag_r.at[d, z_hi, j], device)

    def onward(j, z_hi):
        d = (z_hi + j) % 2
        return d, (x + 3 + 2 * d) % NX, at(s, zh, (x + 1 + 2 * d) % NX)

    def forward(j, z_hi):
        d, col, device = onward(j, z_hi)
        return remote(g.at[col, j, z_hi], g.at[col, j, z_hi], fw_s.at[z_hi, j], fw_r.at[z_hi, j], device)

    def got_gather(j, d, z_hi):
        col = (x + 3 + 2 * d) % NX
        remote(g.at[col, j, z_hi], g.at[col, j, z_hi], ag_s.at[d, z_hi, j], ag_r.at[d, z_hi, j], right).wait_recv()

    def got_forward(j, z_hi):
        remote(g.at[xo, j, z_hi], g.at[xo, j, z_hi], fw_s.at[z_hi, j], fw_r.at[z_hi, j], right).wait_recv()

    for d in (0, 1):
        far(0, d).start()
    for d in (0, 1):
        near(0, d).start()
    for d in (0, 1):
        far(1, d).start()
    for c in small:
        c.start()
    for c in own_loads[8:]:
        c.start()

    h_one[...] = hadamard_signs(BLOCK, BLOCK)
    h_two[...] = hadamard_signs(2 * BLOCK, 2 * BLOCK).astype(jnp.bfloat16)
    acc[...] = jnp.zeros_like(acc)
    ssq[...] = jnp.zeros_like(ssq)

    @pl.when(s == 0)
    def _():
        g[x] = jnp.zeros(g.shape[1:], g.dtype)

    def combine(j):
        for d in (0, 1):
            own_loads[4 * j + d].wait()
            far(j, d).wait_recv()
            ab[d, j] = (ab[d, j].astype(jnp.float32) + pv[d, j].astype(jnp.float32)).astype(jnp.bfloat16)
            comb(j, d).start()

    def gathered_sum(j, z_hi):
        return (
            rsb[z_hi, 0, j].astype(jnp.float32)
            + rsb[z_hi, 1, j].astype(jnp.float32)
            + pv[2 + z_hi, j].astype(jnp.float32)
        )

    def exchange(j):
        own_loads[4 * j + 2].wait()
        own_loads[4 * j + 3].wait()
        for d in (0, 1):
            near(j, d).wait_recv()
            comb(j, d).wait_recv()
        zs[j] = gathered_sum(j, 1 - zh).astype(jnp.bfloat16)
        pair(j).start()

    def row(ref, b):
        return ref[pl.ds(b, 1), :]

    def encode(j):
        pair(j).wait_recv()
        summed = (
            gathered_sum(j, zh)
            + zr[j].astype(jnp.float32)
            + rv[:, j * width : (j + 1) * width].astype(jnp.float32)
        )
        e = jnp.swapaxes(expo[...], 0, 1)
        for q in range(0, blocks, 2):
            b = t * (own // BLOCK) + j * blocks + q
            sgn = jnp.concatenate([row(signs, b), row(signs, b + 1)], axis=1)
            sgn = (2 * sgn - 1).astype(jnp.float32)
            value = summed[:, q * BLOCK : (q + 2) * BLOCK] * sgn
            high = value.astype(jnp.bfloat16)
            rest = value - high.astype(jnp.float32)
            mid = rest.astype(jnp.bfloat16)
            low = (rest - mid.astype(jnp.float32)).astype(jnp.bfloat16)
            h = h_two[...]
            turned = (
                jnp.dot(low, h, preferred_element_type=jnp.float32)
                + jnp.dot(mid, h, preferred_element_type=jnp.float32)
                + jnp.dot(high, h, preferred_element_type=jnp.float32)
            ) * norm_h
            for r in (0, 1):
                k = j * blocks + q + r
                column = jnp.broadcast_to(e[:, k : k + 1], (tok, BLOCK))
                scaled = turned[:, r * BLOCK : (r + 1) * BLOCK] * power_table(column, -1)
                coded = jnp.clip(scaled, -clip_level, clip_level).astype(jnp.bfloat16)
                ys[j, :, (q + r) * BLOCK : (q + r + 1) * BLOCK] = (
                    coded.astype(jnp.float32) * power_table(column, 1)
                ).astype(jnp.bfloat16)

        if j % 2 == 0:

            @pl.when(s < n_sec - 1)
            def _():
                hand(j).start()

        else:

            @pl.when((s < n_sec - 1) & (closing == 0))
            def _():
                hand(j).start()

            @pl.when(closing == 1)
            def _():
                detour(j).start()

    def step_aside(j):
        @pl.when(between == 1)
        def _():
            remote(rb.at[j // 2], rb.at[j // 2], d_s.at[j // 2], d_r.at[j // 2], right).wait_recv()
            detour_on(j).start()

    def fold_weights(j):
        def body(i, carry):
            b = (i // blocks) * (own // BLOCK) + j * blocks + i % blocks
            scale = (2 * row(signs, b) - 1).astype(jnp.float32) * row(gain, b)
            turn = h_one[...] * scale
            high = turn.astype(jnp.bfloat16)
            low = (turn - high.astype(jnp.float32)).astype(jnp.bfloat16)
            rows = pl.ds(pl.multiple_of(b * BLOCK, BLOCK), BLOCK)
            w = jnp.concatenate([wv[0, rows, :], wv[1, rows, :]], axis=1)
            prod = jnp.dot(
                jnp.concatenate([high, low], axis=1),
                jnp.concatenate([w, w], axis=0),
                preferred_element_type=jnp.float32,
            )
            wp[rows, :] = (prod * norm_h).astype(jnp.bfloat16)
            return carry

        lax.fori_loop(0, 2 * NX * blocks, body, 0, unroll=2)

    def arrived(j, z_hi):
        remote(g.at[x, j, z_hi], g.at[x, j, z_hi], c_s.at[j], y_r.at[z_hi, j], right).wait_recv()

    def relay(j):
        @pl.when(s > 0)
        def _():
            relay_across(j).start()

    def spread(j):
        @pl.when(s > 0)
        def _():
            arrived(j, zh)

        for d in (0, 1):
            gather(j, d, zh).start()

    def spread_other(j):
        @pl.when(s > 0)
        def _():
            arrived(j, 1 - zh)

        for d in (0, 1):
            gather(j, d, 1 - zh).start()

    def pass_on(j, z_hi):
        d, _, _ = onward(j, z_hi)
        got_gather(j, d, z_hi)
        forward(j, z_hi).start()

    def project(j, col, z_hi):
        v = g[col, j, z_hi]
        rows = pl.ds(pl.multiple_of((z_hi * NX + col) * own + j * width, width), width)
        acc[...] += jnp.dot(v, wp[rows, :], preferred_element_type=jnp.float32)
        f = v.astype(jnp.float32)
        sq = f * f
        total = sq[:, :BLOCK]
        for q in range(1, blocks):
            total = total + sq[:, q * BLOCK : (q + 1) * BLOCK]
        ssq[...] += total

    def send_on(j):
        if j < slices:
            for d in (0, 1):
                near(j, d).start()
        if j + 1 < slices:
            for d in (0, 1):
                far(j + 1, d).start()

    def project_near(j, z_hi):
        d, col, _ = onward(j, z_hi)
        project(j, x, z_hi)
        project(j, col, z_hi)
        got_gather(j, 1 - d, z_hi)
        project(j, (x + 1 + 2 * d) % NX, z_hi)

    def project_far(j, z_hi):
        got_forward(j, z_hi)
        project(j, xo, z_hi)

    def sent_sums(k):
        for d in (0, 1):
            far(k, d).wait_send()
            near(k, d).wait_send()
            comb(k, d).wait_send()
        pair(k).wait_send()

    def sent_gather(j, z_hi):
        forward(j, z_hi).wait_send()
        for d in (0, 1):
            gather(j, d, z_hi).wait_send()

    for k in range(slices):
        combine(k)
        send_on(k + 1)
        if k == slices - 1:
            spread(0)
            spread(1)
        if k == 0:
            for c in small:
                c.wait()
        if k >= 1:
            exchange(k - 1)
        if k >= 3:
            encode(k - 3)
        if k == 6:
            step_aside(1)
        fold_weights(k)

    for step in TAIL:
        kind, k = step[0], int(step[1:])
        if kind == "X":
            exchange(k)
        elif kind == "E":
            encode(k)
        elif kind == "D":
            step_aside(k)
        elif kind == "R":
            relay(k)
        elif kind == "S":
            spread(k)
        elif kind == "O":
            spread_other(k)
        elif kind in "PQ":
            pass_on(k, zh if kind == "P" else 1 - zh)
        elif kind in "NM":
            project_near(k, zh if kind == "N" else 1 - zh)
            if kind == "N":
                sent_sums(k)
        elif kind in "FG":
            z_hi = zh if kind == "F" else 1 - zh
            project_far(k, z_hi)
            sent_gather(k, z_hi)

    @pl.when(s < n_sec - 1)
    def _():
        for j in range(slices):
            hand(j).wait_send()

    @pl.when(s > 0)
    def _():
        for j in range(slices):
            relay_across(j).wait_send()

    @pl.when(between == 1)
    def _():
        for j in range(1, slices, 2):
            detour_on(j).wait_send()

    mean = jnp.sum(ssq[...], axis=1, keepdims=True) * jnp.float32(1.0 / (2 * NX * own))
    result = acc[...] * lax.rsqrt(mean + norm_eps)
    out[0, 0] = result[:, :BLOCK].astype(out.dtype)
    out[0, 1] = result[:, BLOCK:].astype(out.dtype)


def on_device(partials, residual, exponents, signs, gain, kv_weight):
    tok, own = residual.shape[1], residual.shape[2]
    model = signs.shape[0]
    c = SLICES
    width = own // c
    bf, f32 = jnp.bfloat16, jnp.float32
    dma = pltpu.SemaphoreType.DMA
    blocks2d = (model // BLOCK, BLOCK)
    return pl.pallas_call(
        kernel,
        out_shape=jax.ShapeDtypeStruct((1, 2, tok, kv_weight.shape[3]), bf),
        in_specs=[pl.BlockSpec(memory_space=pl.ANY)] * 6,
        out_specs=pl.BlockSpec(memory_space=pltpu.VMEM),
        scratch_shapes=[
            pltpu.VMEM((4, c, tok, width), bf),
            pltpu.VMEM((2, c, tok, width), bf),
            pltpu.VMEM((2, 2, c, tok, width), bf),
            pltpu.VMEM((c, tok, width), bf),
            pltpu.VMEM((c, tok, width), bf),
            pltpu.VMEM((c, tok, width), bf),
            pltpu.VMEM((c // 2, tok, width), bf),
            pltpu.VMEM((NX, c, 2, tok, width), bf),
            pltpu.VMEM((2, model, BLOCK), bf),
            pltpu.VMEM((model, 2 * BLOCK), bf),
            pltpu.VMEM((tok, own), bf),
            pltpu.VMEM((own // BLOCK, tok), jnp.int32),
            pltpu.VMEM(blocks2d, jnp.int32),
            pltpu.VMEM(blocks2d, f32),
            pltpu.VMEM((BLOCK, BLOCK), f32),
            pltpu.VMEM((2 * BLOCK, 2 * BLOCK), bf),
            pltpu.VMEM((tok, 2 * BLOCK), f32),
            pltpu.VMEM((tok, BLOCK), f32),
            dma((4, c)),
            dma((6,)),
            dma((2, c)),
            dma((2, c)),
            dma((2, c)),
            dma((2, c)),
            dma((2, 2, c)),
            dma((c,)),
            dma((c,)),
            dma((c,)),
            dma((2, c)),
            dma((c,)),
            dma((c // 2,)),
            dma((c // 2,)),
            dma((2, 2, c)),
            dma((2, 2, c)),
            dma((2, c)),
            dma((2, c)),
        ],
        compiler_params=pltpu.CompilerParams(
            collective_id=0, has_side_effects=True, vmem_limit_bytes=62 << 20
        ),
        cost_estimate=pl.CostEstimate(
            flops=6 * tok * model * 2 * BLOCK, bytes_accessed=14 << 20, transcendentals=tok
        ),
        name="relay",
    )(partials, residual, jnp.swapaxes(exponents, 1, 2), signs.reshape(blocks2d), gain.reshape(blocks2d), kv_weight)


def solution(mesh):
    placed = (
        P("section", "tensor", "dp", None),
        P("section", "dp", "tensor"),
        P("section", "dp", "tensor"),
        P(),
        P(),
        P("section", None, None, "tensor"),
    )
    return jax.shard_map(
        on_device,
        mesh=mesh,
        in_specs=placed,
        out_specs=P("section", None, "dp", "tensor"),
        check_vma=False,
    )
```

```python
import functools
import math

import jax
import jax.numpy as jnp
from jax import lax
from jax.experimental import pallas as pl
from jax.experimental.pallas import tpu as pltpu
from jax.sharding import PartitionSpec as P

MESH = pl.DeviceIdType.MESH
BLOCK = 128
clip_level = 448.0
exp_low = -8
exp_high = -3
norm_eps = 1e-05
SLICES = 8
TAIL = (
    "S2", "D3", "S3", "X7", "E5", "P0", "P1", "E6", "S4", "R0", "P2", "D5", "S5", "R1",
    "E7", "P3", "S6", "R2", "N0", "P4", "D7", "S7", "R3", "N1", "P5", "R4", "N2", "R5",
    "P6", "N3", "R6", "O0", "P7", "R7", "N4", "O1", "F0", "F1", "N5", "O2", "Q0", "F2",
    "F3", "N6", "O3", "Q1", "F4", "F5", "N7", "O4", "Q2", "F6", "F7", "M0", "O5", "Q3",
    "M1", "G0", "O6", "Q4", "M2", "G1", "O7", "Q5", "M3", "G2", "Q6", "M4", "G3", "M5",
    "Q7", "G4", "M6", "G5", "M7", "G6", "G7",
)
NX = 4
NY = 4


def power_table(exponents_in, direction):
    factor = jnp.zeros(exponents_in.shape, jnp.float32)
    for power_level in range(exp_low, exp_high):
        factor = factor + jnp.where(
            exponents_in == power_level,
            jnp.float32(2.0 ** (direction * power_level)),
            jnp.float32(0.0),
        )
    return factor


def hadamard_signs(rows, cols):
    i = lax.broadcasted_iota(jnp.int32, (rows, cols), 0)
    j = lax.broadcasted_iota(jnp.int32, (rows, cols), 1)
    p = (i & j) & (BLOCK - 1)
    p = p ^ (p >> 4)
    p = p ^ (p >> 2)
    p = p ^ (p >> 1)
    signs = (1 - 2 * (p & 1)).astype(jnp.float32)
    return jnp.where((i >> 7) == (j >> 7), signs, 0.0)


def kernel(
    part, resid, expo_h, signs_h, gain_h, w_h, out,
    pv, ab, rsb, zs, zr, ys, rb, g, wv, wp, rv, expo, signs, gain, h_one, h_two, acc, ssq,
    pv_s, in_s, a_s, a_r, raw_s, comb_s, rs_r, z_s, z_r, y_s, y_r, c_s, d_s, d_r, ag_s, ag_r, fw_s, fw_r,
):
    n_sec = lax.axis_size("section")
    s, dp, t = lax.axis_index("section"), lax.axis_index("dp"), lax.axis_index("tensor")
    zh, x = t // NX, t % NX
    xr, xl, xo = (x + 1) % NX, (x + 3) % NX, (x + 2) % NX
    tok, slices, width = pv.shape[2], pv.shape[1], pv.shape[3]
    own = slices * width
    blocks = width // BLOCK
    closing = (s % NY) // (NY - 1) * ((2 * n_sec - 2 - s) // n_sec)
    first = 1 - (s % NY + NY - 1) // NY
    between = first * (1 - s // (n_sec - NY))
    opening = first * ((s + n_sec - 1) // n_sec)
    norm_h = jnp.float32(1.0 / math.sqrt(BLOCK))

    def at(section, z_hi, col):
        return (section, dp, z_hi * NX + col)

    right, left, across = at(s, zh, xr), at(s, zh, xl), at(s, 1 - zh, x)

    def cols(z_hi, col, j):
        return pl.ds(pl.multiple_of((z_hi * NX + col) * own + j * width, width), width)

    own_loads = []
    for j in range(slices):
        for k, (z_hi, col) in enumerate(((0, xr), (1, xl), (0, x), (1, x))):
            own_loads.append(
                pltpu.make_async_copy(part.at[0, 0, :, cols(z_hi, col, j)], pv.at[k, j], pv_s.at[k, j])
            )
    small = [
        pltpu.make_async_copy(expo_h.at[0], expo, in_s.at[0]),
        pltpu.make_async_copy(signs_h, signs, in_s.at[1]),
        pltpu.make_async_copy(gain_h, gain, in_s.at[2]),
        pltpu.make_async_copy(resid.at[0], rv, in_s.at[3]),
        pltpu.make_async_copy(w_h.at[0, 0], wv.at[0], in_s.at[4]),
        pltpu.make_async_copy(w_h.at[0, 1], wv.at[1], in_s.at[5]),
    ]
    bar = pltpu.get_barrier_semaphore()

    def greet(device):
        pl.semaphore_signal(bar, inc=1, device_id=device, device_id_type=MESH)

    for device in (right, left, across):
        greet(device)

    @pl.when(s > 0)
    def _():
        greet(at(s - 1, zh, x))

    @pl.when(s < n_sec - 1)
    def _():
        greet(at(s + 1, zh, x))

    @pl.when(closing == 1)
    def _():
        greet(at(s - (NY - 1), zh, x))

    @pl.when(between == 1)
    def _():
        greet(at(s + NY - 1, zh, x))
        greet(at(s + NY, zh, x))

    @pl.when(opening == 1)
    def _():
        greet(at(s - NY, zh, x))

    before = (s + n_sec - 1) // n_sec
    after = (2 * n_sec - 2 - s) // n_sec
    for c in own_loads[:8]:
        c.start()
    pl.semaphore_wait(bar, 3 + before + after + closing + 2 * between + opening)

    def remote(src, dst, send, recv, device):
        return pltpu.make_async_remote_copy(
            src_ref=src, dst_ref=dst, send_sem=send, recv_sem=recv, device_id=device, device_id_type=MESH
        )

    def far(j, d):
        z_hi, device = (0, right) if d == 0 else (1, left)
        return remote(part.at[0, 0, :, cols(z_hi, xo, j)], ab.at[d, j], a_s.at[d, j], a_r.at[d, j], device)

    def near(j, d):
        z_hi, col, device = (1, xr, right) if d == 0 else (0, xl, left)
        return remote(
            part.at[0, 0, :, cols(z_hi, col, j)], rsb.at[z_hi, d, j], raw_s.at[d, j], rs_r.at[z_hi, d, j], device
        )

    def comb(j, d):
        device = right if d == 0 else left
        return remote(ab.at[d, j], rsb.at[d, d, j], comb_s.at[d, j], rs_r.at[d, d, j], device)

    def pair(j):
        return remote(zs.at[j], zr.at[j], z_s.at[j], z_r.at[j], across)

    def hand(j):
        return remote(ys.at[j], g.at[x, j, zh], y_s.at[j], y_r.at[zh, j], at(s + 1, zh, x))

    def detour(j):
        return remote(ys.at[j], rb.at[j // 2], y_s.at[j], d_r.at[j // 2], at(s - (NY - 1), zh, x))

    def detour_on(j):
        return remote(rb.at[j // 2], g.at[x, j, zh], d_s.at[j // 2], y_r.at[zh, j], at(s + NY, zh, x))

    def relay_across(j):
        return remote(g.at[x, j, zh], g.at[x, j, zh], c_s.at[j], y_r.at[zh, j], across)

    def gather(j, d, z_hi):
        device = right if d == 0 else left
        return remote(g.at[x, j, z_hi], g.at[x, j, z_hi], ag_s.at[d, z_hi, j], ag_r.at[d, z_hi, j], device)

    def onward(j, z_hi):
        d = (z_hi + j) % 2
        return d, (x + 3 + 2 * d) % NX, at(s, zh, (x + 1 + 2 * d) % NX)

    def forward(j, z_hi):
        d, col, device = onward(j, z_hi)
        return remote(g.at[col, j, z_hi], g.at[col, j, z_hi], fw_s.at[z_hi, j], fw_r.at[z_hi, j], device)

    def got_gather(j, d, z_hi):
        col = (x + 3 + 2 * d) % NX
        remote(g.at[col, j, z_hi], g.at[col, j, z_hi], ag_s.at[d, z_hi, j], ag_r.at[d, z_hi, j], right).wait_recv()

    def got_forward(j, z_hi):
        remote(g.at[xo, j, z_hi], g.at[xo, j, z_hi], fw_s.at[z_hi, j], fw_r.at[z_hi, j], right).wait_recv()

    for d in (0, 1):
        far(0, d).start()
    for d in (0, 1):
        near(0, d).start()
    for d in (0, 1):
        far(1, d).start()
    for c in small:
        c.start()
    for c in own_loads[8:]:
        c.start()

    h_one[...] = hadamard_signs(BLOCK, BLOCK)
    h_two[...] = hadamard_signs(2 * BLOCK, 2 * BLOCK).astype(jnp.bfloat16)
    acc[...] = jnp.zeros_like(acc)
    ssq[...] = jnp.zeros_like(ssq)

    @pl.when(s == 0)
    def _():
        g[x] = jnp.zeros(g.shape[1:], g.dtype)

    def combine(j):
        for d in (0, 1):
            own_loads[4 * j + d].wait()
            far(j, d).wait_recv()
            ab[d, j] = (ab[d, j].astype(jnp.float32) + pv[d, j].astype(jnp.float32)).astype(jnp.bfloat16)
            comb(j, d).start()

    def gathered_sum(j, z_hi):
        return (
            rsb[z_hi, 0, j].astype(jnp.float32)
            + rsb[z_hi, 1, j].astype(jnp.float32)
            + pv[2 + z_hi, j].astype(jnp.float32)
        )

    def exchange(j):
        own_loads[4 * j + 2].wait()
        own_loads[4 * j + 3].wait()
        for d in (0, 1):
            near(j, d).wait_recv()
            comb(j, d).wait_recv()
        zs[j] = gathered_sum(j, 1 - zh).astype(jnp.bfloat16)
        pair(j).start()

    def row(ref, b):
        return ref[pl.ds(b, 1), :]

    def encode(j):
        pair(j).wait_recv()
        summed = (
            gathered_sum(j, zh)
            + zr[j].astype(jnp.float32)
            + rv[:, j * width : (j + 1) * width].astype(jnp.float32)
        )
        e = jnp.swapaxes(expo[...], 0, 1)
        for q in range(0, blocks, 2):
            b = t * (own // BLOCK) + j * blocks + q
            sgn = jnp.concatenate([row(signs, b), row(signs, b + 1)], axis=1)
            sgn = (2 * sgn - 1).astype(jnp.float32)
            value = summed[:, q * BLOCK : (q + 2) * BLOCK] * sgn
            high = value.astype(jnp.bfloat16)
            rest = value - high.astype(jnp.float32)
            mid = rest.astype(jnp.bfloat16)
            low = (rest - mid.astype(jnp.float32)).astype(jnp.bfloat16)
            h = h_two[...]
            turned = (
                jnp.dot(low, h, preferred_element_type=jnp.float32)
                + jnp.dot(mid, h, preferred_element_type=jnp.float32)
                + jnp.dot(high, h, preferred_element_type=jnp.float32)
            ) * norm_h
            for r in (0, 1):
                k = j * blocks + q + r
                column = jnp.broadcast_to(e[:, k : k + 1], (tok, BLOCK))
                scaled = turned[:, r * BLOCK : (r + 1) * BLOCK] * power_table(column, -1)
                coded = jnp.clip(scaled, -clip_level, clip_level).astype(jnp.bfloat16)
                ys[j, :, (q + r) * BLOCK : (q + r + 1) * BLOCK] = (
                    coded.astype(jnp.float32) * power_table(column, 1)
                ).astype(jnp.bfloat16)

        if j % 2 == 0:

            @pl.when(s < n_sec - 1)
            def _():
                hand(j).start()

        else:

            @pl.when((s < n_sec - 1) & (closing == 0))
            def _():
                hand(j).start()

            @pl.when(closing == 1)
            def _():
                detour(j).start()

    def step_aside(j):
        @pl.when(between == 1)
        def _():
            remote(rb.at[j // 2], rb.at[j // 2], d_s.at[j // 2], d_r.at[j // 2], right).wait_recv()
            detour_on(j).start()

    def fold_weights(j):
        def body(i, carry):
            b = (i // blocks) * (own // BLOCK) + j * blocks + i % blocks
            scale = (2 * row(signs, b) - 1).astype(jnp.float32) * row(gain, b)
            turn = h_one[...] * scale
            high = turn.astype(jnp.bfloat16)
            low = (turn - high.astype(jnp.float32)).astype(jnp.bfloat16)
            rows = pl.ds(pl.multiple_of(b * BLOCK, BLOCK), BLOCK)
            w = jnp.concatenate([wv[0, rows, :], wv[1, rows, :]], axis=1)
            prod = jnp.dot(
                jnp.concatenate([high, low], axis=1),
                jnp.concatenate([w, w], axis=0),
                preferred_element_type=jnp.float32,
            )
            wp[rows, :] = (prod * norm_h).astype(jnp.bfloat16)
            return carry

        lax.fori_loop(0, 2 * NX * blocks, body, 0, unroll=2)

    def arrived(j, z_hi):
        remote(g.at[x, j, z_hi], g.at[x, j, z_hi], c_s.at[j], y_r.at[z_hi, j], right).wait_recv()

    def relay(j):
        @pl.when(s > 0)
        def _():
            relay_across(j).start()

    def spread(j):
        @pl.when(s > 0)
        def _():
            arrived(j, zh)

        for d in (0, 1):
            gather(j, d, zh).start()

    def spread_other(j):
        @pl.when(s > 0)
        def _():
            arrived(j, 1 - zh)

        for d in (0, 1):
            gather(j, d, 1 - zh).start()

    def pass_on(j, z_hi):
        d, _, _ = onward(j, z_hi)
        got_gather(j, d, z_hi)
        forward(j, z_hi).start()

    def project(j, col, z_hi):
        v = g[col, j, z_hi]
        rows = pl.ds(pl.multiple_of((z_hi * NX + col) * own + j * width, width), width)
        acc[...] += jnp.dot(v, wp[rows, :], preferred_element_type=jnp.float32)
        f = v.astype(jnp.float32)
        sq = f * f
        total = sq[:, :BLOCK]
        for q in range(1, blocks):
            total = total + sq[:, q * BLOCK : (q + 1) * BLOCK]
        ssq[...] += total

    def send_on(j):
        if j < slices:
            for d in (0, 1):
                near(j, d).start()
        if j + 1 < slices:
            for d in (0, 1):
                far(j + 1, d).start()

    def project_near(j, z_hi):
        d, col, _ = onward(j, z_hi)
        project(j, x, z_hi)
        project(j, col, z_hi)
        got_gather(j, 1 - d, z_hi)
        project(j, (x + 1 + 2 * d) % NX, z_hi)

    def project_far(j, z_hi):
        got_forward(j, z_hi)
        project(j, xo, z_hi)

    def sent_sums(k):
        for d in (0, 1):
            far(k, d).wait_send()
            near(k, d).wait_send()
            comb(k, d).wait_send()
        pair(k).wait_send()

    def sent_gather(j, z_hi):
        forward(j, z_hi).wait_send()
        for d in (0, 1):
            gather(j, d, z_hi).wait_send()

    for k in range(slices):
        combine(k)
        send_on(k + 1)
        if k == slices - 1:
            spread(0)
            spread(1)
        if k == 0:
            for c in small:
                c.wait()
        if k >= 1:
            exchange(k - 1)
        if k >= 3:
            encode(k - 3)
        if k == 6:
            step_aside(1)
        fold_weights(k)

    for step in TAIL:
        kind, k = step[0], int(step[1:])
        if kind == "X":
            exchange(k)
        elif kind == "E":
            encode(k)
        elif kind == "D":
            step_aside(k)
        elif kind == "R":
            relay(k)
        elif kind == "S":
            spread(k)
        elif kind == "O":
            spread_other(k)
        elif kind in "PQ":
            pass_on(k, zh if kind == "P" else 1 - zh)
        elif kind in "NM":
            project_near(k, zh if kind == "N" else 1 - zh)
            if kind == "N":
                sent_sums(k)
        elif kind in "FG":
            z_hi = zh if kind == "F" else 1 - zh
            project_far(k, z_hi)
            if k >= 3:
                sent_gather(k - 3, z_hi)

    @pl.when(s < n_sec - 1)
    def _():
        for j in range(slices):
            hand(j).wait_send()

    @pl.when(s > 0)
    def _():
        for j in range(slices):
            relay_across(j).wait_send()

    @pl.when(between == 1)
    def _():
        for j in range(1, slices, 2):
            detour_on(j).wait_send()

    for k in range(slices - 3, slices):
        for z_hi in (zh, 1 - zh):
            sent_gather(k, z_hi)
    mean = jnp.sum(ssq[...], axis=1, keepdims=True) * jnp.float32(1.0 / (2 * NX * own))
    result = acc[...] * lax.rsqrt(mean + norm_eps)
    out[0, 0] = result[:, :BLOCK].astype(out.dtype)
    out[0, 1] = result[:, BLOCK:].astype(out.dtype)


def on_device(partials, residual, exponents, signs, gain, kv_weight):
    tok, own = residual.shape[1], residual.shape[2]
    model = signs.shape[0]
    c = SLICES
    width = own // c
    bf, f32 = jnp.bfloat16, jnp.float32
    dma = pltpu.SemaphoreType.DMA
    blocks2d = (model // BLOCK, BLOCK)
    return pl.pallas_call(
        kernel,
        out_shape=jax.ShapeDtypeStruct((1, 2, tok, kv_weight.shape[3]), bf),
        in_specs=[pl.BlockSpec(memory_space=pl.ANY)] * 6,
        out_specs=pl.BlockSpec(memory_space=pltpu.VMEM),
        scratch_shapes=[
            pltpu.VMEM((4, c, tok, width), bf),
            pltpu.VMEM((2, c, tok, width), bf),
            pltpu.VMEM((2, 2, c, tok, width), bf),
            pltpu.VMEM((c, tok, width), bf),
            pltpu.VMEM((c, tok, width), bf),
            pltpu.VMEM((c, tok, width), bf),
            pltpu.VMEM((c // 2, tok, width), bf),
            pltpu.VMEM((NX, c, 2, tok, width), bf),
            pltpu.VMEM((2, model, BLOCK), bf),
            pltpu.VMEM((model, 2 * BLOCK), bf),
            pltpu.VMEM((tok, own), bf),
            pltpu.VMEM((own // BLOCK, tok), jnp.int32),
            pltpu.VMEM(blocks2d, jnp.int32),
            pltpu.VMEM(blocks2d, f32),
            pltpu.VMEM((BLOCK, BLOCK), f32),
            pltpu.VMEM((2 * BLOCK, 2 * BLOCK), bf),
            pltpu.VMEM((tok, 2 * BLOCK), f32),
            pltpu.VMEM((tok, BLOCK), f32),
            dma((4, c)),
            dma((6,)),
            dma((2, c)),
            dma((2, c)),
            dma((2, c)),
            dma((2, c)),
            dma((2, 2, c)),
            dma((c,)),
            dma((c,)),
            dma((c,)),
            dma((2, c)),
            dma((c,)),
            dma((c // 2,)),
            dma((c // 2,)),
            dma((2, 2, c)),
            dma((2, 2, c)),
            dma((2, c)),
            dma((2, c)),
        ],
        compiler_params=pltpu.CompilerParams(
            collective_id=0, has_side_effects=True, vmem_limit_bytes=62 << 20
        ),
        cost_estimate=pl.CostEstimate(
            flops=6 * tok * model * 2 * BLOCK, bytes_accessed=14 << 20, transcendentals=tok
        ),
        name="relay",
    )(partials, residual, jnp.swapaxes(exponents, 1, 2), signs.reshape(blocks2d), gain.reshape(blocks2d), kv_weight)


def solution(mesh):
    placed = (
        P("section", "tensor", "dp", None),
        P("section", "dp", "tensor"),
        P("section", "dp", "tensor"),
        P(),
        P(),
        P("section", None, None, "tensor"),
    )
    return jax.shard_map(
        on_device,
        mesh=mesh,
        in_specs=placed,
        out_specs=P("section", None, "dp", "tensor"),
        check_vma=False,
    )
```

```python
import functools
import math

import jax
import jax.numpy as jnp
from jax import lax
from jax.experimental import pallas as pl
from jax.experimental.pallas import tpu as pltpu
from jax.sharding import PartitionSpec as P

MESH = pl.DeviceIdType.MESH
BLOCK = 128
clip_level = 448.0
exp_low = -8
exp_high = -3
norm_eps = 1e-05
SLICES = 8
TAIL = (
    "S2", "D3", "S3", "X7", "E5", "P0", "P1", "E6", "S4", "R0", "P2", "D5", "S5", "R1",
    "E7", "P3", "S6", "R2", "N0", "P4", "D7", "S7", "R3", "N1", "P5", "R4", "N2", "R5",
    "P6", "N3", "R6", "O0", "P7", "R7", "N4", "O1", "F0", "F1", "N5", "O2", "Q0", "F2",
    "F3", "N6", "O3", "Q1", "F4", "F5", "N7", "O4", "Q2", "F6", "F7", "M0", "O5", "Q3",
    "M1", "G0", "O6", "Q4", "M2", "G1", "O7", "Q5", "M3", "G2", "Q6", "M4", "G3", "M5",
    "Q7", "G4", "M6", "G5", "M7", "G6", "G7",
)
NX = 4
NY = 4


def power_table(exponents_in, direction):
    factor = jnp.zeros(exponents_in.shape, jnp.float32)
    for power_level in range(exp_low, exp_high):
        factor = factor + jnp.where(
            exponents_in == power_level,
            jnp.float32(2.0 ** (direction * power_level)),
            jnp.float32(0.0),
        )
    return factor


def hadamard_signs(rows, cols):
    i = lax.broadcasted_iota(jnp.int32, (rows, cols), 0)
    j = lax.broadcasted_iota(jnp.int32, (rows, cols), 1)
    p = (i & j) & (BLOCK - 1)
    p = p ^ (p >> 4)
    p = p ^ (p >> 2)
    p = p ^ (p >> 1)
    signs = (1 - 2 * (p & 1)).astype(jnp.float32)
    return jnp.where((i >> 7) == (j >> 7), signs, 0.0)


def kernel(
    part, resid, expo_h, signs_h, gain_h, w_h, out,
    pv, ab, rsb, zs, zr, ys, rb, g, wv, wp, rv, expo, signs, gain, h_one, h_two, acc, ssq,
    pv_s, in_s, a_s, a_r, raw_s, comb_s, rs_r, z_s, z_r, y_s, y_r, c_s, d_s, d_r, ag_s, ag_r, fw_s, fw_r,
):
    n_sec = lax.axis_size("section")
    s, dp, t = lax.axis_index("section"), lax.axis_index("dp"), lax.axis_index("tensor")
    zh, x = t // NX, t % NX
    xr, xl, xo = (x + 1) % NX, (x + 3) % NX, (x + 2) % NX
    tok, slices, width = pv.shape[2], pv.shape[1], pv.shape[3]
    own = slices * width
    blocks = width // BLOCK
    closing = (s % NY) // (NY - 1) * ((2 * n_sec - 2 - s) // n_sec)
    first = 1 - (s % NY + NY - 1) // NY
    between = first * (1 - s // (n_sec - NY))
    opening = first * ((s + n_sec - 1) // n_sec)
    norm_h = jnp.float32(1.0 / math.sqrt(BLOCK))

    def at(section, z_hi, col):
        return (section, dp, z_hi * NX + col)

    right, left, across = at(s, zh, xr), at(s, zh, xl), at(s, 1 - zh, x)

    def cols(z_hi, col, j):
        return pl.ds(pl.multiple_of((z_hi * NX + col) * own + j * width, width), width)

    own_loads = []
    for j in range(slices):
        for k, (z_hi, col) in enumerate(((0, xr), (1, xl), (0, x), (1, x))):
            own_loads.append(
                pltpu.make_async_copy(part.at[0, 0, :, cols(z_hi, col, j)], pv.at[k, j], pv_s.at[k, j])
            )
    small = [
        pltpu.make_async_copy(expo_h.at[0], expo, in_s.at[0]),
        pltpu.make_async_copy(signs_h, signs, in_s.at[1]),
        pltpu.make_async_copy(gain_h, gain, in_s.at[2]),
        pltpu.make_async_copy(resid.at[0], rv, in_s.at[3]),
        pltpu.make_async_copy(w_h.at[0, 0], wv.at[0], in_s.at[4]),
        pltpu.make_async_copy(w_h.at[0, 1], wv.at[1], in_s.at[5]),
    ]
    bar = pltpu.get_barrier_semaphore()

    def greet(device):
        pl.semaphore_signal(bar, inc=1, device_id=device, device_id_type=MESH)

    for device in (right, left, across):
        greet(device)

    @pl.when(s > 0)
    def _():
        greet(at(s - 1, zh, x))

    @pl.when(s < n_sec - 1)
    def _():
        greet(at(s + 1, zh, x))

    @pl.when(closing == 1)
    def _():
        greet(at(s - (NY - 1), zh, x))

    @pl.when(between == 1)
    def _():
        greet(at(s + NY - 1, zh, x))
        greet(at(s + NY, zh, x))

    @pl.when(opening == 1)
    def _():
        greet(at(s - NY, zh, x))

    before = (s + n_sec - 1) // n_sec
    after = (2 * n_sec - 2 - s) // n_sec
    for c in own_loads[:8]:
        c.start()
    pl.semaphore_wait(bar, 3 + before + after + closing + 2 * between + opening)

    def remote(src, dst, send, recv, device):
        return pltpu.make_async_remote_copy(
            src_ref=src, dst_ref=dst, send_sem=send, recv_sem=recv, device_id=device, device_id_type=MESH
        )

    def far(j, d):
        z_hi, device = (0, right) if d == 0 else (1, left)
        return remote(part.at[0, 0, :, cols(z_hi, xo, j)], ab.at[d, j], a_s.at[d, j], a_r.at[d, j], device)

    def near(j, d):
        z_hi, col, device = (1, xr, right) if d == 0 else (0, xl, left)
        return remote(
            part.at[0, 0, :, cols(z_hi, col, j)], rsb.at[z_hi, d, j], raw_s.at[d, j], rs_r.at[z_hi, d, j], device
        )

    def comb(j, d):
        device = right if d == 0 else left
        return remote(ab.at[d, j], rsb.at[d, d, j], comb_s.at[d, j], rs_r.at[d, d, j], device)

    def pair(j):
        return remote(zs.at[j], zr.at[j], z_s.at[j], z_r.at[j], across)

    def hand(j):
        return remote(ys.at[j], g.at[x, j, zh], y_s.at[j], y_r.at[zh, j], at(s + 1, zh, x))

    def detour(j):
        return remote(ys.at[j], rb.at[j // 2], y_s.at[j], d_r.at[j // 2], at(s - (NY - 1), zh, x))

    def detour_on(j):
        return remote(rb.at[j // 2], g.at[x, j, zh], d_s.at[j // 2], y_r.at[zh, j], at(s + NY, zh, x))

    def relay_across(j):
        return remote(g.at[x, j, zh], g.at[x, j, zh], c_s.at[j], y_r.at[zh, j], across)

    def gather(j, d, z_hi):
        device = right if d == 0 else left
        return remote(g.at[x, j, z_hi], g.at[x, j, z_hi], ag_s.at[d, z_hi, j], ag_r.at[d, z_hi, j], device)

    def onward(j, z_hi):
        d = (z_hi + j) % 2
        return d, (x + 3 + 2 * d) % NX, at(s, zh, (x + 1 + 2 * d) % NX)

    def forward(j, z_hi):
        d, col, device = onward(j, z_hi)
        return remote(g.at[col, j, z_hi], g.at[col, j, z_hi], fw_s.at[z_hi, j], fw_r.at[z_hi, j], device)

    def got_gather(j, d, z_hi):
        col = (x + 3 + 2 * d) % NX
        remote(g.at[col, j, z_hi], g.at[col, j, z_hi], ag_s.at[d, z_hi, j], ag_r.at[d, z_hi, j], right).wait_recv()

    def got_forward(j, z_hi):
        remote(g.at[xo, j, z_hi], g.at[xo, j, z_hi], fw_s.at[z_hi, j], fw_r.at[z_hi, j], right).wait_recv()

    for d in (0, 1):
        far(0, d).start()
    for d in (0, 1):
        near(0, d).start()
    for d in (0, 1):
        far(1, d).start()
    for c in small:
        c.start()
    for c in own_loads[8:]:
        c.start()

    h_one[...] = hadamard_signs(BLOCK, BLOCK)
    h_two[...] = hadamard_signs(2 * BLOCK, 2 * BLOCK).astype(jnp.bfloat16)
    acc[...] = jnp.zeros_like(acc)
    ssq[...] = jnp.zeros_like(ssq)

    @pl.when(s == 0)
    def _():
        g[x] = jnp.zeros(g.shape[1:], g.dtype)

    def combine(j):
        for d in (0, 1):
            own_loads[4 * j + d].wait()
            far(j, d).wait_recv()
            ab[d, j] = (ab[d, j].astype(jnp.float32) + pv[d, j].astype(jnp.float32)).astype(jnp.bfloat16)
            comb(j, d).start()

    def gathered_sum(j, z_hi):
        return (
            rsb[z_hi, 0, j].astype(jnp.float32)
            + rsb[z_hi, 1, j].astype(jnp.float32)
            + pv[2 + z_hi, j].astype(jnp.float32)
        )

    def exchange(j):
        own_loads[4 * j + 2].wait()
        own_loads[4 * j + 3].wait()
        for d in (0, 1):
            near(j, d).wait_recv()
            comb(j, d).wait_recv()
        zs[j] = gathered_sum(j, 1 - zh).astype(jnp.bfloat16)

        @pl.when(s < n_sec - 1)
        def _():
            pair(j).start()

    def row(ref, b):
        return ref[pl.ds(b, 1), :]

    def encode(j):
        pl.when(s < n_sec - 1)(lambda: pair(j).wait_recv())
        summed = (
            gathered_sum(j, zh)
            + zr[j].astype(jnp.float32)
            + rv[:, j * width : (j + 1) * width].astype(jnp.float32)
        )
        e = jnp.swapaxes(expo[...], 0, 1)
        for q in range(0, blocks, 2):
            b = t * (own // BLOCK) + j * blocks + q
            sgn = jnp.concatenate([row(signs, b), row(signs, b + 1)], axis=1)
            sgn = (2 * sgn - 1).astype(jnp.float32)
            value = summed[:, q * BLOCK : (q + 2) * BLOCK] * sgn
            high = value.astype(jnp.bfloat16)
            rest = value - high.astype(jnp.float32)
            mid = rest.astype(jnp.bfloat16)
            low = (rest - mid.astype(jnp.float32)).astype(jnp.bfloat16)
            h = h_two[...]
            turned = (
                jnp.dot(low, h, preferred_element_type=jnp.float32)
                + jnp.dot(mid, h, preferred_element_type=jnp.float32)
                + jnp.dot(high, h, preferred_element_type=jnp.float32)
            ) * norm_h
            for r in (0, 1):
                k = j * blocks + q + r
                column = jnp.broadcast_to(e[:, k : k + 1], (tok, BLOCK))
                scaled = turned[:, r * BLOCK : (r + 1) * BLOCK] * power_table(column, -1)
                coded = jnp.clip(scaled, -clip_level, clip_level).astype(jnp.bfloat16)
                ys[j, :, (q + r) * BLOCK : (q + r + 1) * BLOCK] = (
                    coded.astype(jnp.float32) * power_table(column, 1)
                ).astype(jnp.bfloat16)

        if j % 2 == 0:

            @pl.when(s < n_sec - 1)
            def _():
                hand(j).start()

        else:

            @pl.when((s < n_sec - 1) & (closing == 0))
            def _():
                hand(j).start()

            @pl.when(closing == 1)
            def _():
                detour(j).start()

    def step_aside(j):
        @pl.when(between == 1)
        def _():
            remote(rb.at[j // 2], rb.at[j // 2], d_s.at[j // 2], d_r.at[j // 2], right).wait_recv()
            detour_on(j).start()

    def fold_weights(j):
        def body(i, carry):
            b = (i // blocks) * (own // BLOCK) + j * blocks + i % blocks
            scale = (2 * row(signs, b) - 1).astype(jnp.float32) * row(gain, b)
            turn = h_one[...] * scale
            high = turn.astype(jnp.bfloat16)
            low = (turn - high.astype(jnp.float32)).astype(jnp.bfloat16)
            rows = pl.ds(pl.multiple_of(b * BLOCK, BLOCK), BLOCK)
            w = jnp.concatenate([wv[0, rows, :], wv[1, rows, :]], axis=1)
            prod = jnp.dot(
                jnp.concatenate([high, low], axis=1),
                jnp.concatenate([w, w], axis=0),
                preferred_element_type=jnp.float32,
            )
            wp[rows, :] = (prod * norm_h).astype(jnp.bfloat16)
            return carry

        lax.fori_loop(0, 2 * NX * blocks, body, 0, unroll=2)

    def arrived(j, z_hi):
        remote(g.at[x, j, z_hi], g.at[x, j, z_hi], c_s.at[j], y_r.at[z_hi, j], right).wait_recv()

    def relay(j):
        @pl.when(s > 0)
        def _():
            relay_across(j).start()

    def spread(j):
        @pl.when(s > 0)
        def _():
            arrived(j, zh)

        for d in (0, 1):
            gather(j, d, zh).start()

    def spread_other(j):
        @pl.when(s > 0)
        def _():
            arrived(j, 1 - zh)

        for d in (0, 1):
            gather(j, d, 1 - zh).start()

    def pass_on(j, z_hi):
        d, _, _ = onward(j, z_hi)
        got_gather(j, d, z_hi)
        forward(j, z_hi).start()

    def project(j, col, z_hi):
        v = g[col, j, z_hi]
        rows = pl.ds(pl.multiple_of((z_hi * NX + col) * own + j * width, width), width)
        acc[...] += jnp.dot(v, wp[rows, :], preferred_element_type=jnp.float32)
        f = v.astype(jnp.float32)
        sq = f * f
        total = sq[:, :BLOCK]
        for q in range(1, blocks):
            total = total + sq[:, q * BLOCK : (q + 1) * BLOCK]
        ssq[...] += total

    def send_on(j):
        if j < slices:
            for d in (0, 1):
                near(j, d).start()
        if j + 1 < slices:
            for d in (0, 1):
                far(j + 1, d).start()

    def project_near(j, z_hi):
        d, col, _ = onward(j, z_hi)
        project(j, x, z_hi)
        project(j, col, z_hi)
        got_gather(j, 1 - d, z_hi)
        project(j, (x + 1 + 2 * d) % NX, z_hi)

    def project_far(j, z_hi):
        got_forward(j, z_hi)
        project(j, xo, z_hi)

    def sent_sums(k):
        for d in (0, 1):
            far(k, d).wait_send()
            near(k, d).wait_send()
            comb(k, d).wait_send()
        pl.when(s < n_sec - 1)(lambda: pair(k).wait_send())

    def sent_gather(j, z_hi):
        forward(j, z_hi).wait_send()
        for d in (0, 1):
            gather(j, d, z_hi).wait_send()

    for k in range(slices):
        combine(k)
        send_on(k + 1)
        if k == slices - 1:
            spread(0)
            spread(1)
        if k == 0:
            for c in small:
                c.wait()
        if k >= 1:
            exchange(k - 1)
        if k >= 3:
            encode(k - 3)
        if k == 6:
            step_aside(1)
        fold_weights(k)

    for step in TAIL:
        kind, k = step[0], int(step[1:])
        if kind == "X":
            exchange(k)
        elif kind == "E":
            encode(k)
        elif kind == "D":
            step_aside(k)
        elif kind == "R":
            relay(k)
        elif kind == "S":
            spread(k)
        elif kind == "O":
            spread_other(k)
        elif kind in "PQ":
            pass_on(k, zh if kind == "P" else 1 - zh)
        elif kind in "NM":
            project_near(k, zh if kind == "N" else 1 - zh)
            if kind == "N":
                sent_sums(k)
        elif kind in "FG":
            z_hi = zh if kind == "F" else 1 - zh
            project_far(k, z_hi)
            if k >= 3:
                sent_gather(k - 3, z_hi)

    @pl.when(s < n_sec - 1)
    def _():
        for j in range(slices):
            hand(j).wait_send()

    @pl.when(s > 0)
    def _():
        for j in range(slices):
            relay_across(j).wait_send()

    @pl.when(between == 1)
    def _():
        for j in range(1, slices, 2):
            detour_on(j).wait_send()

    for k in range(slices - 3, slices):
        for z_hi in (zh, 1 - zh):
            sent_gather(k, z_hi)
    mean = jnp.sum(ssq[...], axis=1, keepdims=True) * jnp.float32(1.0 / (2 * NX * own))
    result = acc[...] * lax.rsqrt(mean + norm_eps)
    out[0, 0] = result[:, :BLOCK].astype(out.dtype)
    out[0, 1] = result[:, BLOCK:].astype(out.dtype)


def on_device(partials, residual, exponents, signs, gain, kv_weight):
    tok, own = residual.shape[1], residual.shape[2]
    model = signs.shape[0]
    c = SLICES
    width = own // c
    bf, f32 = jnp.bfloat16, jnp.float32
    dma = pltpu.SemaphoreType.DMA
    blocks2d = (model // BLOCK, BLOCK)
    return pl.pallas_call(
        kernel,
        out_shape=jax.ShapeDtypeStruct((1, 2, tok, kv_weight.shape[3]), bf),
        in_specs=[pl.BlockSpec(memory_space=pl.ANY)] * 6,
        out_specs=pl.BlockSpec(memory_space=pltpu.VMEM),
        scratch_shapes=[
            pltpu.VMEM((4, c, tok, width), bf),
            pltpu.VMEM((2, c, tok, width), bf),
            pltpu.VMEM((2, 2, c, tok, width), bf),
            pltpu.VMEM((c, tok, width), bf),
            pltpu.VMEM((c, tok, width), bf),
            pltpu.VMEM((c, tok, width), bf),
            pltpu.VMEM((c // 2, tok, width), bf),
            pltpu.VMEM((NX, c, 2, tok, width), bf),
            pltpu.VMEM((2, model, BLOCK), bf),
            pltpu.VMEM((model, 2 * BLOCK), bf),
            pltpu.VMEM((tok, own), bf),
            pltpu.VMEM((own // BLOCK, tok), jnp.int32),
            pltpu.VMEM(blocks2d, jnp.int32),
            pltpu.VMEM(blocks2d, f32),
            pltpu.VMEM((BLOCK, BLOCK), f32),
            pltpu.VMEM((2 * BLOCK, 2 * BLOCK), bf),
            pltpu.VMEM((tok, 2 * BLOCK), f32),
            pltpu.VMEM((tok, BLOCK), f32),
            dma((4, c)),
            dma((6,)),
            dma((2, c)),
            dma((2, c)),
            dma((2, c)),
            dma((2, c)),
            dma((2, 2, c)),
            dma((c,)),
            dma((c,)),
            dma((c,)),
            dma((2, c)),
            dma((c,)),
            dma((c // 2,)),
            dma((c // 2,)),
            dma((2, 2, c)),
            dma((2, 2, c)),
            dma((2, c)),
            dma((2, c)),
        ],
        compiler_params=pltpu.CompilerParams(
            collective_id=0, has_side_effects=True, vmem_limit_bytes=62 << 20
        ),
        cost_estimate=pl.CostEstimate(
            flops=6 * tok * model * 2 * BLOCK, bytes_accessed=14 << 20, transcendentals=tok
        ),
        name="relay",
    )(partials, residual, jnp.swapaxes(exponents, 1, 2), signs.reshape(blocks2d), gain.reshape(blocks2d), kv_weight)


def solution(mesh):
    placed = (
        P("section", "tensor", "dp", None),
        P("section", "dp", "tensor"),
        P("section", "dp", "tensor"),
        P(),
        P(),
        P("section", None, None, "tensor"),
    )
    return jax.shard_map(
        on_device,
        mesh=mesh,
        in_specs=placed,
        out_specs=P("section", None, "dp", "tensor"),
        check_vma=False,
    )
```
